256 devices in a mesh: nodes: 64 (over x, z, core), feat: 4 (over y).
Axes of the slice: x: 4, y: 4, z: 8, core: 2. Of those that a mesh axis runs over, the one named last changes fastest.
Arguments:
- x_t: bfloat16 [128, 131072], P('feat', 'nodes'), may hold values from -6 to 6
- weight: bfloat16 [128, 256], P(None, 'feat'), may hold values from -0.5 to 0.5
- cotangent: bfloat16 [256, 131072], P('feat', 'nodes'), may hold values from -6 to 6
- self_tiles: bfloat16 [1024, 128, 128], P('nodes'), may hold values from -0.125 to 0.125
- hub_tiles: bfloat16 [1024, 8, 128, 128], P('nodes'), may hold values from -0.125 to 0.125
- nbr_tiles: bfloat16 [1024, 8, 128, 128], P('nodes'), may hold values from -0.125 to 0.125
- hub_ids: int32 [8], replicated, may hold values from 0 to 1023
- send_list: int32 [64, 64, 2], P('nodes'), may hold values from 0 to 15
- nbr_slot: int32 [64, 128], P('nodes'), may hold values from 0 to 127, each once within a row
Outputs:
- activation: bfloat16 [256, 131072], P('feat', 'nodes')
- weight_grad: float32 [128, 256], P(None, 'feat')
- input_grad: float32 [128, 131072], P('feat', 'nodes')
The draws below stay inside these ranges and needn't reach their ends.
Inputs may be any that keep to these rules, and one draw needn't show every extreme that they name: `nbr_slot`: each row is a permutation of 0 to 127: every received slot feeds exactly one tile. `hub_ids`: hub numbers may repeat.
All inputs are finite; a program needn't handle non-finite values.
Results may differ from the reference program's by a relative error of at most 0.0057.
Values may be sent and summed in bfloat16 or wider, within the bound.
No kernel may reach another device: no remote copies, remote signals or barrier semaphores. Data moves between devices by JAX's collectives and lax.ppermute only.
A program may use at most 64 MiB of HBM per device.

```python
import jax
import jax.numpy as jnp
from jax import lax

FIN = 128
HID = 256
BLOCK = 128
BLK_DEV = 16
HUBS = 8
SLOTS = 2
NBR = 8
BLOCKS = 1024
NODES = 131072
N_NODES = 64


def set_ends(values, stream_key, low, top_value):
    spot = [jax.random.randint(jax.random.fold_in(stream_key, axis), (), 0, length) for axis, length in enumerate(values.shape)]
    widest = values.shape.index(max(values.shape))
    next_to = spot[:widest] + [(spot[widest] + 1) % values.shape[widest]] + spot[widest + 1:]
    return values.at[tuple(spot)].set(low).at[tuple(next_to)].set(top_value)


def block_levels(stream_key, shape, split, smallest, high):
    factor_of = 1.0
    for position, parts in split:
        draws = jax.random.uniform(jax.random.fold_in(jax.random.fold_in(stream_key, 6), position), (parts,), jnp.float32, smallest / len(split), high / len(split))
        factor_of = factor_of * jnp.repeat(jnp.exp(draws), shape[position] // parts).reshape((-1,) + (1,) * (len(shape) - 1 - position))
    return factor_of


def centred(own_key, shape, width, reach, shards=(), kind=jnp.bfloat16):
    entries = jax.random.normal(own_key, shape, jnp.float32) * width
    if len(shards) > 0:
        entries = block_levels(own_key, shape, shards, -0.22, 0.18) * entries
    return jnp.clip(entries, min=-reach, max=reach).astype(kind)


def setup_inputs(seed: int = 0) -> dict:
    keys = jax.random.split(jax.random.key(seed), 10)
    x_t = centred(keys[0], (FIN, NODES), 1.0, 6.0, ((0, 4), (1, 64)))
    weight = centred(keys[1], (FIN, HID), FIN ** -0.5, 0.5, ((1, 4),))
    cotangent = centred(keys[2], (HID, NODES), 1.0, 6.0, ((0, 4), (1, 64)))
    self_tiles = centred(keys[3], (BLOCKS, BLOCK, BLOCK), (BLOCK * (1 + HUBS + NBR)) ** -0.5, 0.125, ((0, 64),))
    hub_tiles = centred(keys[4], (BLOCKS, HUBS, BLOCK, BLOCK), (BLOCK * (1 + HUBS + NBR)) ** -0.5, 0.125, ((0, 64),))
    nbr_tiles = centred(keys[5], (BLOCKS, NBR, BLOCK, BLOCK), (BLOCK * (1 + HUBS + NBR)) ** -0.5, 0.125, ((0, 64),))
    hub_ids = set_ends(jax.random.randint(keys[6], (HUBS,), 0, BLOCKS), jax.random.fold_in(keys[6], 1), 0, BLOCKS - 1).astype(jnp.int32)
    send_list = set_ends(jax.random.randint(keys[7], (N_NODES, N_NODES, SLOTS), 0, BLK_DEV), jax.random.fold_in(keys[7], 1), 0, BLK_DEV - 1).astype(jnp.int32)
    nbr_slot = jax.vmap(lambda own: jax.random.permutation(own, N_NODES * SLOTS))(jax.random.split(keys[8], N_NODES)).reshape((N_NODES, N_NODES * SLOTS)).astype(jnp.int32)
    return dict(x_t=x_t, weight=weight, cotangent=cotangent, self_tiles=self_tiles, hub_tiles=hub_tiles, nbr_tiles=nbr_tiles, hub_ids=hub_ids, send_list=send_list, nbr_slot=nbr_slot)


def silu_slope(pre):
    sig = jax.nn.sigmoid(pre)
    return sig * (1.0 + pre * (1.0 - sig))


def reference(x_t, weight, cotangent, self_tiles, hub_tiles, nbr_tiles, hub_ids, send_list, nbr_slot):
    x_blocks = x_t.reshape(FIN, BLOCKS, BLOCK)
    slot_ids = jnp.arange(N_NODES * SLOTS, dtype=jnp.int32)
    senders = slot_ids // SLOTS
    slot_part = slot_ids % SLOTS
    readers = jnp.arange(N_NODES, dtype=jnp.int32)
    by_slot = senders[None, :] * BLK_DEV + send_list[senders[None, :], readers[:, None], slot_part[None, :]]
    source = jnp.take_along_axis(by_slot, nbr_slot, axis=1).reshape(BLOCKS, NBR).astype(jnp.int32)
    hub_x = jnp.take(x_blocks, hub_ids, axis=1).astype(jnp.float32)

    def one_block(dest):
        near = jnp.take(x_blocks, source[dest], axis=1).astype(jnp.float32)
        total = jnp.einsum('fjs,jsd->fd', near, nbr_tiles[dest].astype(jnp.float32))
        total = total + jnp.einsum('fhs,hsd->fd', hub_x, hub_tiles[dest].astype(jnp.float32))
        own = lax.dynamic_index_in_dim(x_blocks, dest, 1, keepdims=False)
        total = total + jnp.dot(own, self_tiles[dest], preferred_element_type=jnp.float32)
        return total

    agg_blocks = lax.map(one_block, jnp.arange(BLOCKS, dtype=jnp.int32))
    aggregated = jnp.transpose(agg_blocks, (1, 0, 2)).reshape(FIN, NODES).astype(jnp.bfloat16)
    pre = lax.dot_general(weight, aggregated, (((0,), (0,)), ((), ())), preferred_element_type=jnp.float32)
    activation = jax.nn.silu(pre).astype(jnp.bfloat16)
    pre_grad = (cotangent.astype(jnp.float32) * silu_slope(pre)).astype(jnp.bfloat16)
    weight_grad = lax.dot_general(aggregated, pre_grad, (((1,), (1,)), ((), ())), preferred_element_type=jnp.float32)
    agg_grad = jnp.dot(weight, pre_grad, preferred_element_type=jnp.float32).astype(jnp.bfloat16)
    grad_blocks = agg_grad.reshape(FIN, BLOCKS, BLOCK)

    def scatter_step(carry, dest):
        upstream = lax.dynamic_index_in_dim(grad_blocks, dest, 1, keepdims=False).astype(jnp.float32)
        near = jnp.einsum('fd,jsd->fjs', upstream, nbr_tiles[dest].astype(jnp.float32))
        carry = carry.at[:, source[dest]].add(near)
        hubs = jnp.einsum('fd,hsd->fhs', upstream, hub_tiles[dest].astype(jnp.float32))
        carry = carry.at[:, hub_ids].add(hubs)
        own = jnp.einsum('fd,sd->fs', upstream, self_tiles[dest].astype(jnp.float32))
        carry = carry.at[:, dest].add(own)
        return carry, None

    start = jnp.zeros((FIN, BLOCKS, BLOCK), jnp.float32)
    input_blocks, unused = lax.scan(scatter_step, start, jnp.arange(BLOCKS, dtype=jnp.int32))
    input_grad = input_blocks.reshape(FIN, NODES)
    return activation, weight_grad, input_grad
```

```python
import jax
import jax.numpy as jnp
from jax import lax
from jax.sharding import PartitionSpec as P

BF = jnp.bfloat16
F32 = jnp.float32


def silu_slope(pre):
    sig = jax.nn.sigmoid(pre)
    return sig * (1.0 + pre * (1.0 - sig))


def swap(values):
    return lax.all_to_all(values, "nodes", split_axis=0, concat_axis=0, tiled=True)


def shift(values, step):
    count = lax.axis_size("feat")
    return lax.ppermute(values, "feat", [(i, (i + step) % count) for i in range(count)])


def spread(piece):
    count = lax.axis_size("nodes")
    return swap(jnp.broadcast_to(piece[None], (count,) + piece.shape))


def per_device(
    x_t, weight, cotangent, self_tiles, hub_tiles, nbr_tiles, hub_ids, send_list, nbr_slot
):
    quarter = x_t.shape[0]
    blk_count, block_len = self_tiles.shape[0], self_tiles.shape[1]
    hubs, nbrs = hub_tiles.shape[1], nbr_tiles.shape[1]
    count = lax.axis_size("nodes")
    feats = lax.axis_size("feat")
    row = lax.axis_index("feat")
    me = lax.axis_index("nodes")
    sends = send_list[0].reshape(-1)
    slots = nbr_slot[0]
    per_pair = 2 * quarter

    blocks = x_t.reshape(quarter, blk_count, block_len).transpose(1, 0, 2)
    picked = jnp.take(blocks, sends, axis=0, mode="clip").reshape(count, per_pair, block_len)
    mine = hub_ids // blk_count == me
    panel = jnp.where(mine[:, None, None], jnp.take(blocks, hub_ids % blk_count, axis=0, mode="clip"), 0)
    panel = panel.reshape(count, -1, block_len)
    got = swap(jnp.concatenate([picked, panel], axis=1))
    hub_piece = jnp.sum(got[:, per_pair:].astype(F32), axis=0).astype(BF)
    hub_x = spread(hub_piece).reshape(hubs, quarter, block_len)
    slot_x = got[:, :per_pair].reshape(-1, quarter, block_len)
    chosen = jnp.take(slot_x, slots, axis=0, mode="clip").reshape(blk_count, nbrs, quarter, block_len)
    total = jnp.einsum("bjfs,bjsd->bfd", chosen, nbr_tiles, preferred_element_type=F32)
    total = total + jnp.einsum("bfs,bsd->bfd", blocks, self_tiles, preferred_element_type=F32)
    total = total + jnp.einsum("hfs,bhsd->bfd", hub_x, hub_tiles, preferred_element_type=F32)
    own_agg = total.astype(BF).transpose(1, 0, 2).reshape(quarter, blk_count * block_len)

    agg = jnp.concatenate([own_agg] + [shift(own_agg, k) for k in range(1, feats)], axis=0)
    weight_rows = weight.reshape(feats, quarter, -1)
    order = (row - jnp.arange(feats, dtype=jnp.int32)) % feats
    turned = jnp.take(weight_rows, order, axis=0, mode="clip").reshape(weight.shape)
    pre = lax.dot_general(turned, agg, (((0,), (0,)), ((), ())), preferred_element_type=F32)
    activation = jax.nn.silu(pre).astype(BF)
    pre_grad = (cotangent.astype(F32) * silu_slope(pre)).astype(BF)
    weight_part = lax.dot_general(
        agg, pre_grad, (((1,), (1,)), ((), ())), preferred_element_type=F32
    )
    weight_part = jnp.take(weight_part.reshape(feats, quarter, -1), order, axis=0, mode="clip")
    parts = jnp.dot(turned, pre_grad, preferred_element_type=F32)
    parts = parts.reshape(feats, quarter, -1)
    upstream = parts[0]
    for k in range(1, feats):
        upstream = upstream + shift(parts[k].astype(BF), feats - k).astype(F32)
    upstream = upstream.astype(BF).reshape(quarter, blk_count, block_len).transpose(1, 0, 2)

    near = jnp.einsum("bfd,bjsd->bjfs", upstream, nbr_tiles, preferred_element_type=F32)
    near = near.astype(BF).reshape(blk_count * nbrs, quarter, block_len)
    tile_of = jnp.zeros_like(slots).at[slots].set(jnp.arange(slots.shape[0], dtype=slots.dtype))
    placed = jnp.take(near, tile_of, axis=0, mode="clip").reshape(count, per_pair, block_len)
    hub_terms = jnp.einsum("bfd,bhsd->hfs", upstream, hub_tiles, preferred_element_type=F32)
    hub_terms = hub_terms.astype(BF).reshape(count, -1, block_len)
    hub_rows = hub_terms.shape[1]
    weight_part = weight_part.astype(BF).reshape(count, -1, block_len)
    back = swap(jnp.concatenate([placed, hub_terms, weight_part], axis=1))
    sums = jnp.sum(back[:, per_pair:].astype(F32), axis=0)
    sums = spread(sums)
    hub_total = sums[:, :hub_rows].reshape(hubs, quarter, block_len)
    weight_grad = sums[:, hub_rows:].reshape(weight.shape)
    returned = back[:, :per_pair].reshape(-1, quarter, block_len)
    own = jnp.einsum("bfd,bsd->bfs", upstream, self_tiles, preferred_element_type=F32)
    ids = jnp.arange(blk_count, dtype=jnp.int32)
    send_select = (sends[:, None] == ids[None, :]).astype(BF)
    own = own + jnp.einsum("rfs,rb->bfs", returned, send_select, preferred_element_type=F32)
    hub_select = (hub_ids[:, None] == me * blk_count + ids[None, :]).astype(F32)
    own = own + jnp.einsum(
        "hfs,hb->bfs", hub_total, hub_select, precision=lax.Precision.HIGHEST
    )
    input_grad = own.transpose(1, 0, 2).reshape(quarter, blk_count * block_len)
    return (activation, weight_grad, input_grad)


def solution(mesh):
    return jax.shard_map(
        per_device,
        mesh=mesh,
        in_specs=(
            P("feat", "nodes"),
            P(None, "feat"),
            P("feat", "nodes"),
            P("nodes", None, None),
            P("nodes", None, None, None),
            P("nodes", None, None, None),
            P(),
            P("nodes", None, None),
            P("nodes", None),
        ),
        out_specs=(P("feat", "nodes"), P(None, "feat"), P("feat", "nodes")),
        check_vma=False,
    )
```

```python
import jax
import jax.numpy as jnp
from jax import lax
from jax.sharding import PartitionSpec as P

BF = jnp.bfloat16
F32 = jnp.float32
I32 = jnp.int32
XS, ZS, CS = 4, 8, 2
NEAR, FAR = (0, 1, 7, 2, 6), (3, 5, 4)
GROUPS = (NEAR, FAR)


def silu_slope(pre):
    sig = jax.nn.sigmoid(pre)
    return sig * (1.0 + pre * (1.0 - sig))


def node(x, z, core):
    return (x % XS * ZS + z % ZS) * CS + core % CS


def hop(values, x=0, z=0, core=0):
    pairs = [
        (node(i, j, k), node(i + x, j + z, k + core))
        for i in range(XS)
        for j in range(ZS)
        for k in range(CS)
    ]
    return lax.ppermute(values, "nodes", pairs)


def pair_swap(values, x=0, z=0, core=0):
    pairs = [
        (node(i, j, k), node(i ^ x, j ^ z, k ^ core))
        for i in range(XS)
        for j in range(ZS)
        for k in range(CS)
    ]
    return lax.ppermute(values, "nodes", pairs)


def shift(values, step):
    count = lax.axis_size("feat")
    return lax.ppermute(values, "feat", [(i, (i + step) % count) for i in range(count)])


def pick(values, ids):
    return jnp.take(values, ids, axis=0, mode="clip")


def per_distance(numbers, distance):
    return pick(jnp.array(numbers, I32), distance)


def per_device(
    x_t, weight, cotangent, self_tiles, hub_tiles, nbr_tiles, hub_ids, send_list, nbr_slot
):
    quarter = x_t.shape[0]
    blk_count, block_len = self_tiles.shape[0], self_tiles.shape[1]
    hubs, nbrs = hub_tiles.shape[1], nbr_tiles.shape[1]
    feats = lax.axis_size("feat")
    row = lax.axis_index("feat")
    me = lax.axis_index("nodes")
    my_x, my_z, my_core = me // (ZS * CS), me // CS % ZS, me % CS
    slots = nbr_slot[0]
    per_pair = send_list.shape[2]

    blocks = x_t.reshape(quarter, blk_count, block_len).transpose(1, 0, 2)
    lists = send_list.reshape(1, 1, -1).astype(BF)
    lists = jnp.pad(lists, ((0, 0), (0, quarter - 1), (0, 0)))
    payload = jnp.concatenate([blocks, lists], axis=0)
    column = {0: payload}
    for d in (3, 5, 4, 2, 6, 1, 7)[::-1]:
        column[d] = hop(payload, z=d)

    group_of = [0] * ZS
    place_of = [0] * ZS
    for g, ds in enumerate(GROUPS):
        for i, d in enumerate(ds):
            group_of[d], place_of[d] = g, i
    group_len = [len(GROUPS[g]) for g in group_of]
    start_of = [len(NEAR) * XS * CS * per_pair * g for g in group_of]
    readers = ((my_x + jnp.arange(XS, dtype=I32)) % XS * ZS + my_z) * CS + my_core
    hub_dev, hub_blk = hub_ids // blk_count, hub_ids % blk_count
    hub_far = (my_z - hub_dev // CS % ZS) % ZS
    hub_here = hub_dev // (ZS * CS) == my_x
    hub_cell = (hub_dev % CS + my_core) % CS * per_distance(group_len, hub_far)
    hub_cell = hub_cell + per_distance(place_of, hub_far)
    hub_group = per_distance(group_of, hub_far)

    arrived = []
    cells = []
    panel = jnp.zeros((hubs, quarter, block_len), BF)
    for g, ds in enumerate(GROUPS):
        n = len(ds)
        side = jnp.stack([column[d] for d in ds])
        table = jnp.concatenate([side, hop(side, core=1)], axis=0)
        wanted = table[:, blk_count, 0].astype(I32).reshape(CS * n, -1, per_pair)
        wanted = jnp.take(wanted, readers, axis=1, mode="clip")
        wanted = wanted.transpose(1, 0, 2)
        cell = jnp.arange(CS * n, dtype=I32)[None, :, None]
        cells.append((cell * blk_count + wanted).reshape(-1))
        table = table.reshape(-1, quarter, block_len)
        found = pick(table, (cell * (blk_count + 1) + wanted).reshape(-1))
        inside = hub_here & (hub_group == g)
        hub_found = pick(table, hub_cell * (blk_count + 1) + hub_blk)
        panel = jnp.where(inside[:, None, None], hub_found, panel)
        found = found.reshape(XS, -1, quarter, block_len)
        if g == len(GROUPS) - 1:
            own_panel = panel
            hub_x = panel.astype(F32)
        parts = [found[0]]
        for e in range(1, XS):
            if g == len(GROUPS) - 1:
                came = hop(jnp.concatenate([found[e], own_panel], axis=0), x=e)
                hub_x = hub_x + came[-hubs:].astype(F32)
                came = came[:-hubs]
            else:
                came = hop(found[e], x=e)
            parts.append(came)
        arrived += parts
    arrived = jnp.concatenate(arrived, axis=0)
    hub_x = hub_x.astype(BF)

    sender, slot_part = slots // per_pair, slots % per_pair
    far = (my_z - sender // CS % ZS) % ZS
    spot = (my_x - sender // (ZS * CS)) % XS * CS + (sender + my_core) % CS
    spot = spot * per_distance(group_len, far) + per_distance(place_of, far)
    spot = per_distance(start_of, far) + spot * per_pair + slot_part
    tile_of = jnp.zeros_like(spot).at[spot].set(jnp.arange(spot.shape[0], dtype=I32))

    chosen = pick(arrived, spot).reshape(blk_count, nbrs, quarter, block_len)
    total = jnp.einsum("bfs,bsd->bfd", blocks, self_tiles, preferred_element_type=F32)
    total = total + jnp.einsum("bjfs,bjsd->bfd", chosen, nbr_tiles, preferred_element_type=F32)
    total = total + jnp.einsum("hfs,bhsd->bfd", hub_x, hub_tiles, preferred_element_type=F32)
    own_agg = total.astype(BF).transpose(1, 0, 2).reshape(quarter, blk_count * block_len)

    agg = jnp.concatenate([own_agg] + [shift(own_agg, k) for k in range(1, feats)], axis=0)
    weight_rows = weight.reshape(feats, quarter, -1)
    order = (row - jnp.arange(feats, dtype=I32)) % feats
    turned = pick(weight_rows, order).reshape(weight.shape)
    pre = lax.dot_general(turned, agg, (((0,), (0,)), ((), ())), preferred_element_type=F32)
    activation = jax.nn.silu(pre).astype(BF)
    pre_grad = (cotangent.astype(F32) * silu_slope(pre)).astype(BF)
    parts = jnp.dot(turned, pre_grad, preferred_element_type=F32)
    parts = parts.reshape(feats, quarter, -1)
    upstream = parts[0]
    for k in range(1, feats):
        upstream = upstream + shift(parts[k].astype(BF), feats - k).astype(F32)
    upstream = upstream.astype(BF).reshape(quarter, blk_count, block_len).transpose(1, 0, 2)

    weight_part = lax.dot_general(
        agg, pre_grad, (((1,), (1,)), ((), ())), preferred_element_type=F32
    )
    weight_part = pick(weight_part.reshape(feats, quarter, -1), order)
    weight_grad = weight_part.reshape(-1, 2 * weight.shape[1])
    for step in (dict(core=1), dict(z=1), dict(z=2), dict(z=4), dict(x=1), dict(x=2)):
        weight_grad = weight_grad + pair_swap(weight_grad, **step)
    weight_grad = weight_grad.reshape(weight.shape)

    near = jnp.einsum("bfd,bjsd->bjfs", upstream, nbr_tiles, preferred_element_type=F32)
    near = near.astype(BF).reshape(blk_count * nbrs, quarter, block_len)
    hub_terms = jnp.einsum("bfd,bhsd->hfs", upstream, hub_tiles, preferred_element_type=F32)
    hub_terms = hub_terms.astype(BF)
    placed = pick(near, tile_of)
    own = jnp.einsum("bfd,bsd->bfs", upstream, self_tiles, preferred_element_type=F32)
    hub_back = [hub_terms]
    for g in reversed(range(len(GROUPS))):
        ds = GROUPS[g]
        n = len(ds)
        size = CS * n * per_pair
        first = len(NEAR) * XS * CS * per_pair * g
        terms = [placed[first : first + size]]
        for e in range(1, XS):
            part = placed[first + e * size : first + (e + 1) * size]
            if g == len(GROUPS) - 1:
                came = hop(jnp.concatenate([part, hub_terms], axis=0), x=-e)
                hub_back.append(came[size:])
                came = came[:size]
            else:
                came = hop(part, x=-e)
            terms.append(came)
        terms = jnp.concatenate(terms + hub_back, axis=0)
        inside = hub_here & (hub_group == g)
        hub_col = jnp.where(inside, hub_cell * blk_count + hub_blk, -1)
        target = jnp.concatenate([cells[g]] + [hub_col] * XS)
        select = (target[:, None] == jnp.arange(CS * n * blk_count, dtype=I32)[None, :]).astype(BF)
        sums = jnp.einsum("nfs,nb->bfs", terms, select, preferred_element_type=F32)
        half = n * blk_count
        other = hop(sums[half:].astype(BF), core=1)
        sums = sums[:half] + other.astype(F32)
        for i, d in enumerate(ds):
            mine = sums[i * blk_count : (i + 1) * blk_count]
            if d:
                mine = hop(mine.astype(BF), z=-d).astype(F32)
            own = own + mine
    input_grad = own.transpose(1, 0, 2).reshape(quarter, blk_count * block_len)
    return (activation, weight_grad, input_grad)


def solution(mesh):
    return jax.shard_map(
        per_device,
        mesh=mesh,
        in_specs=(
            P("feat", "nodes"),
            P(None, "feat"),
            P("feat", "nodes"),
            P("nodes", None, None),
            P("nodes", None, None, None),
            P("nodes", None, None, None),
            P(),
            P("nodes", None, None),
            P("nodes", None),
        ),
        out_specs=(P("feat", "nodes"), P(None, "feat"), P("feat", "nodes")),
        check_vma=False,
    )
```

```python
import jax
import jax.numpy as jnp
from jax import lax
from jax.sharding import PartitionSpec as P

BF = jnp.bfloat16
F32 = jnp.float32


def silu_slope(pre):
    sig = jax.nn.sigmoid(pre)
    return sig * (1.0 + pre * (1.0 - sig))


def swap(values):
    return lax.all_to_all(values, "nodes", split_axis=0, concat_axis=0, tiled=True)


def shift(values, step):
    count = lax.axis_size("feat")
    return lax.ppermute(values, "feat", [(i, (i + step) % count) for i in range(count)])


def spread(piece):
    count = lax.axis_size("nodes")
    return swap(jnp.broadcast_to(piece[None], (count,) + piece.shape))


def per_device(
    x_t, weight, cotangent, self_tiles, hub_tiles, nbr_tiles, hub_ids, send_list, nbr_slot
):
    quarter = x_t.shape[0]
    blk_count, block_len = self_tiles.shape[0], self_tiles.shape[1]
    hubs, nbrs = hub_tiles.shape[1], nbr_tiles.shape[1]
    count = lax.axis_size("nodes")
    feats = lax.axis_size("feat")
    row = lax.axis_index("feat")
    me = lax.axis_index("nodes")
    sends = send_list[0].reshape(-1)
    slots = nbr_slot[0]
    per_pair = 2 * quarter

    blocks = x_t.reshape(quarter, blk_count, block_len).transpose(1, 0, 2)
    ids = jnp.arange(blk_count, dtype=jnp.int32)
    wanted = jnp.concatenate([sends, hub_ids - me * blk_count])
    wanted = (wanted[:, None] == ids[None, :]).astype(BF)
    picked = jnp.einsum("nb,bfs->nfs", wanted, blocks, preferred_element_type=F32).astype(BF)
    slots_of = sends.shape[0]
    panel = picked[slots_of:].reshape(count, -1, block_len)
    picked = picked[:slots_of].reshape(count, per_pair, block_len)
    got = swap(jnp.concatenate([picked, panel], axis=1))
    got, slots, row, sends, hub_ids = lax.optimization_barrier((got, slots, row, sends, hub_ids))
    hub_piece = jnp.sum(got[:, per_pair:].astype(F32), axis=0).astype(BF)
    hub_x = spread(hub_piece).reshape(hubs, quarter, block_len)
    slot_x = got[:, :per_pair].reshape(-1, quarter, block_len)
    chosen = jnp.take(slot_x, slots, axis=0, mode="clip").reshape(blk_count, nbrs, quarter, block_len)
    total = jnp.einsum("bjfs,bjsd->bfd", chosen, nbr_tiles, preferred_element_type=F32)
    total = total + jnp.einsum("bfs,bsd->bfd", blocks, self_tiles, preferred_element_type=F32)
    total = total + jnp.einsum("hfs,bhsd->bfd", hub_x, hub_tiles, preferred_element_type=F32)
    own_agg = total.astype(BF).transpose(1, 0, 2).reshape(quarter, blk_count * block_len)

    agg = jnp.concatenate([own_agg] + [shift(own_agg, k) for k in range(1, feats)], axis=0)
    weight_rows = weight.reshape(feats, quarter, -1)
    order = (row - jnp.arange(feats, dtype=jnp.int32)) % feats
    turned = jnp.take(weight_rows, order, axis=0, mode="clip").reshape(weight.shape)
    pre = lax.dot_general(turned, agg, (((0,), (0,)), ((), ())), preferred_element_type=F32)
    activation = jax.nn.silu(pre).astype(BF)
    pre_grad = (cotangent.astype(F32) * silu_slope(pre)).astype(BF)
    weight_part = lax.dot_general(
        agg, pre_grad, (((1,), (1,)), ((), ())), preferred_element_type=F32
    )
    weight_part = jnp.take(weight_part.reshape(feats, quarter, -1), order, axis=0, mode="clip")
    parts = jnp.dot(turned, pre_grad, preferred_element_type=F32)
    parts = parts.reshape(feats, quarter, -1)
    upstream = parts[0]
    for k in range(1, feats):
        upstream = upstream + shift(parts[k].astype(BF), feats - k).astype(F32)
    upstream = upstream.astype(BF).reshape(quarter, blk_count, block_len).transpose(1, 0, 2)

    near = jnp.einsum("bfd,bjsd->bjfs", upstream, nbr_tiles, preferred_element_type=F32)
    near = near.astype(BF).reshape(blk_count * nbrs, quarter, block_len)
    tile_of = jnp.zeros_like(slots).at[slots].set(jnp.arange(slots.shape[0], dtype=slots.dtype))
    placed = jnp.take(near, tile_of, axis=0, mode="clip").reshape(count, per_pair, block_len)
    hub_terms = jnp.einsum("bfd,bhsd->hfs", upstream, hub_tiles, preferred_element_type=F32)
    hub_terms = hub_terms.astype(BF).reshape(count, -1, block_len)
    hub_rows = hub_terms.shape[1]
    weight_part = weight_part.astype(BF).reshape(count, -1, block_len)
    back = swap(jnp.concatenate([placed, hub_terms, weight_part], axis=1))
    sums = jnp.sum(back[:, per_pair:].astype(F32), axis=0)
    sums = spread(sums.astype(BF)).astype(F32)
    hub_total = sums[:, :hub_rows].reshape(hubs, quarter, block_len)
    weight_grad = sums[:, hub_rows:].reshape(weight.shape)
    returned = back[:, :per_pair].reshape(-1, quarter, block_len)
    own = jnp.einsum("bfd,bsd->bfs", upstream, self_tiles, preferred_element_type=F32)
    send_select = (sends[:, None] == ids[None, :]).astype(BF)
    own = own + jnp.einsum("rfs,rb->bfs", returned, send_select, preferred_element_type=F32)
    hub_select = (hub_ids[:, None] == me * blk_count + ids[None, :]).astype(F32)
    own = own + jnp.einsum(
        "hfs,hb->bfs", hub_total, hub_select, precision=lax.Precision.HIGHEST
    )
    input_grad = own.transpose(1, 0, 2).reshape(quarter, blk_count * block_len)
    return (activation, weight_grad, input_grad)


def solution(mesh):
    return jax.shard_map(
        per_device,
        mesh=mesh,
        in_specs=(
            P("feat", "nodes"),
            P(None, "feat"),
            P("feat", "nodes"),
            P("nodes", None, None),
            P("nodes", None, None, None),
            P("nodes", None, None, None),
            P(),
            P("nodes", None, None),
            P("nodes", None),
        ),
        out_specs=(P("feat", "nodes"), P(None, "feat"), P("feat", "nodes")),
        check_vma=False,
    )
```

```python
import jax
import jax.numpy as jnp
from jax import lax
from jax.experimental import pallas as pl
from jax.experimental.pallas import tpu as pltpu
from jax.sharding import PartitionSpec as P

BF = jnp.bfloat16
F32 = jnp.float32


def silu_slope(pre):
    sig = jax.nn.sigmoid(pre)
    return sig * (1.0 + pre * (1.0 - sig))


def swap(values):
    return lax.all_to_all(values, "nodes", split_axis=0, concat_axis=0, tiled=True)


def trade(values, step):
    count = lax.axis_size("feat")
    return lax.ppermute(values, "feat", [(i, i ^ step) for i in range(count)])


def spread(piece):
    count = lax.axis_size("nodes")
    return swap(jnp.broadcast_to(piece[None], (count,) + piece.shape))


TAIL = 8
SMEM = pl.BlockSpec(memory_space=pltpu.SMEM)
VMEM = pl.BlockSpec(memory_space=pltpu.VMEM)


def pack_kernel(numbers_ref, x_ref, msg_ref, tail_ref):
    quarter = x_ref.shape[0]
    count, rows, block_len = msg_ref.shape
    blk_count = x_ref.shape[1] // block_len
    per_dev = (rows - TAIL) // quarter
    hubs = numbers_ref.shape[0] - count * per_dev
    share = hubs * quarter // count

    def columns(block):
        return pl.ds(pl.multiple_of(block * block_len, block_len), block_len)

    def one(r, carry):
        for k in range(per_dev):
            block = numbers_ref[r * per_dev + k]
            msg_ref[r, k * quarter : (k + 1) * quarter, :] = x_ref[:, columns(block)]
        return carry

    lax.fori_loop(0, count, one, 0, unroll=8)
    tail_ref[...] = jnp.zeros_like(tail_ref)
    for h in range(hubs):
        local = numbers_ref[count * per_dev + h]
        inside = (local >= 0) & (local < blk_count)
        values = x_ref[:, columns(jnp.clip(local, 0, blk_count - 1))].astype(F32)
        values = jnp.where(inside, values, 0.0)
        for i in range(quarter // share):
            place = h * (quarter // share) + i
            tail_ref[place, :share, :] = values[i * share : (i + 1) * share]
    msg_ref[:, per_dev * quarter :, :] = tail_ref[...].astype(BF)


def pack(numbers, x_t, count, per_dev, block_len):
    rows = per_dev * x_t.shape[0] + TAIL
    return pl.pallas_call(
        pack_kernel,
        out_shape=jax.ShapeDtypeStruct((count, rows, block_len), BF),
        in_specs=[SMEM, VMEM],
        out_specs=VMEM,
        scratch_shapes=[pltpu.VMEM((count, TAIL, block_len), F32)],
        compiler_params=pltpu.CompilerParams(vmem_limit_bytes=48 << 20),
        name="pack",
    )(numbers, x_t)


def middle_kernel(hub_ref, p0, p1, p2, p3, weight_ref, cot_ref, act_ref, out_ref):
    parts = (p0, p1, p2, p3)
    blks, quarter, block_len = p0.shape
    hid = weight_ref.shape[0] // len(parts)
    weight = weight_ref[...]
    total = jnp.zeros((weight.shape[0], weight.shape[1]), F32)
    for b in range(blks):
        columns = slice(b * block_len, (b + 1) * block_len)
        agg = jnp.concatenate([p[b].astype(F32) for p in parts], axis=0)
        agg = (agg + hub_ref[b]).astype(BF)
        pre = jnp.dot(weight, agg, preferred_element_type=F32)
        sig = jax.nn.sigmoid(pre)
        act_ref[:, columns] = (pre * sig).astype(BF)
        slope = sig * (1.0 + pre * (1.0 - sig))
        pre_grad = (cot_ref[:, columns].astype(F32) * slope).astype(BF)
        agg_grad = lax.dot_general(
            weight, pre_grad, (((0,), (0,)), ((), ())), preferred_element_type=F32
        ).astype(BF)
        for k in range(len(parts)):
            out_ref[k, b * quarter : (b + 1) * quarter, :] = agg_grad[k * quarter : (k + 1) * quarter]
        total = total + lax.dot_general(
            pre_grad, agg, (((1,), (1,)), ((), ())), preferred_element_type=F32
        )
    total = total.astype(BF)
    for k in range(len(parts)):
        out_ref[k, blks * quarter :, :] = total[k * hid : (k + 1) * hid]


def middle(hub_agg, parts, weight, cot):
    blks, quarter, block_len = parts[0].shape
    hid = weight.shape[0] // len(parts)
    return pl.pallas_call(
        middle_kernel,
        out_shape=[
            jax.ShapeDtypeStruct(cot.shape, BF),
            jax.ShapeDtypeStruct((len(parts), blks * quarter + hid, block_len), BF),
        ],
        in_specs=[VMEM] * (3 + len(parts)),
        out_specs=[VMEM, VMEM],
        compiler_params=pltpu.CompilerParams(vmem_limit_bytes=16 << 20),
        cost_estimate=pl.CostEstimate(flops=6 * weight.size * cot.shape[1], transcendentals=cot.size, bytes_accessed=2 << 20),
        name="middle",
    )(hub_agg, *parts, weight, cot)


def finish_kernel(hubs_ref, own_ref, sums_ref, grad_ref, weight_ref, hub_ref):
    quarter = own_ref.shape[0]
    hubs, block_len = hub_ref.shape[0], hub_ref.shape[2]
    blk_count = own_ref.shape[1] // block_len
    count = sums_ref.shape[0]
    share = hubs * quarter // count
    for place in range(count):
        h, i = divmod(place, quarter // share)
        piece = sums_ref[place].astype(F32)
        hub_ref[h, i * share : (i + 1) * share, :] = piece[:share]
        weight_ref[place : place + 1, :] = piece[share : share + 1]
    grad_ref[...] = own_ref[...]
    for h in range(hubs):
        local = hubs_ref[h]

        @pl.when((local >= 0) & (local < blk_count))
        def _():
            first = jnp.clip(local, 0, blk_count - 1) * block_len
            columns = pl.ds(pl.multiple_of(first, block_len), block_len)
            grad_ref[:, columns] += hub_ref[h]


def finish(hubs_here, own, sums, quarter, hid, block_len):
    return pl.pallas_call(
        finish_kernel,
        out_shape=[
            jax.ShapeDtypeStruct(own.shape, F32),
            jax.ShapeDtypeStruct((hid, block_len), F32),
        ],
        in_specs=[SMEM, VMEM, VMEM],
        out_specs=[VMEM, VMEM],
        scratch_shapes=[pltpu.VMEM((hubs_here.shape[0], quarter, block_len), F32)],
        compiler_params=pltpu.CompilerParams(vmem_limit_bytes=16 << 20),
        name="finish",
    )(hubs_here, own, sums)


def per_device(
    x_t, weight, cotangent, self_tiles, hub_tiles, nbr_tiles, hub_ids, send_list, nbr_slot
):
    quarter = x_t.shape[0]
    blk_count, block_len = self_tiles.shape[0], self_tiles.shape[1]
    hubs, nbrs = hub_tiles.shape[1], nbr_tiles.shape[1]
    hid = weight.shape[1]
    count = lax.axis_size("nodes")
    feats = lax.axis_size("feat")
    row = lax.axis_index("feat")
    me = lax.axis_index("nodes")
    sends = send_list[0].reshape(-1)
    slots = nbr_slot[0]
    per_pair = 2 * quarter
    blk_share = blk_count // feats
    share = blk_share * block_len
    steps = jnp.arange(feats, dtype=jnp.int32)

    ids = jnp.arange(blk_count, dtype=jnp.int32)
    hubs_here = hub_ids - me * blk_count
    per_dev = send_list.shape[2]
    got = swap(pack(jnp.concatenate([sends, hubs_here]), x_t, count, per_dev, block_len))

    cot = cotangent.reshape(hid, feats, share)
    cot_parts, weight_parts = [], []
    for k in range(feats):
        part = lax.dynamic_index_in_dim(cot, row ^ k, 1, keepdims=False)
        part = jnp.concatenate([part, weight.T], axis=1)
        part = trade(part, k) if k else part
        cot_parts.append(part[:, :share])
        weight_parts.append(part[:, share:])
    cot_share = jnp.concatenate(cot_parts, axis=0)
    turned = jnp.concatenate(weight_parts, axis=0).reshape(feats * hid, feats, quarter)
    turned = jnp.take(turned, row ^ steps, axis=1, mode="clip")
    feat_ids = jnp.arange(feats * quarter, dtype=jnp.int32)
    owner = row ^ steps[:, None] ^ (feat_ids[None, :] // quarter)
    source = feat_ids[None, :] % quarter + owner * quarter
    unturn = (source[:, None, :] == feat_ids[None, :, None]).astype(BF)

    got, slots, sends, x_t, hubs_here, turned, cot_share, unturn = lax.optimization_barrier(
        (got, slots, sends, x_t, hubs_here, turned, cot_share, unturn)
    )
    blocks = x_t.reshape(quarter, blk_count, block_len).transpose(1, 0, 2)
    hub_rows = hubs * quarter // count
    hub_piece = jnp.sum(got[:, per_pair : per_pair + hub_rows].astype(F32), axis=0).astype(BF)
    hub_piece = jnp.concatenate([hub_piece] + [trade(hub_piece, k) for k in range(1, feats)], axis=0)
    hub_piece, got, blocks = lax.optimization_barrier((hub_piece, got, blocks))
    hub_x = spread(hub_piece).reshape(count, feats, hub_rows, block_len)
    hub_x = hub_x.transpose(1, 0, 2, 3).reshape(feats, hubs, quarter, block_len)

    slot_x = got[:, :per_pair].reshape(-1, quarter, block_len)
    chosen = jnp.take(slot_x, slots, axis=0, mode="clip")
    chosen = chosen.reshape(blk_count, nbrs, quarter, block_len)
    total = jnp.einsum("bjfs,bjsd->bfd", chosen, nbr_tiles, preferred_element_type=F32)
    total = total + jnp.einsum("bfs,bsd->bfd", blocks, self_tiles, preferred_element_type=F32)
    total = total.astype(BF).reshape(feats, blk_share, quarter, block_len)
    parts = []
    for k in range(feats):
        part = lax.dynamic_index_in_dim(total, row ^ k, 0, keepdims=False)
        parts.append(trade(part, k) if k else part)
    hub_share = lax.dynamic_slice_in_dim(hub_tiles, row * blk_share, blk_share, axis=0)
    hub_agg = jnp.einsum("khfs,bhsd->bkfd", hub_x, hub_share, preferred_element_type=F32)
    hub_agg = hub_agg.reshape(blk_share, feats * quarter, block_len)
    act, message = middle(hub_agg, parts, turned.reshape(feats * hid, feats * quarter), cot_share)
    message = jnp.stack([message[0]] + [trade(message[k], k) for k in range(1, feats)])
    upstream = message[:, : blk_share * quarter].reshape(feats, blk_share, quarter, block_len)
    upstream = jnp.take(upstream, row ^ steps, axis=0, mode="clip")
    upstream = upstream.reshape(blk_count, quarter, block_len)
    weight_sum = jnp.einsum(
        "khe,kef->hf", message[:, blk_share * quarter :], unturn, preferred_element_type=F32
    )

    near = jnp.einsum("bfd,bjsd->bjfs", upstream, nbr_tiles, preferred_element_type=F32)
    near = near.astype(BF).reshape(blk_count * nbrs, quarter, block_len)
    tile_of = jnp.zeros_like(slots).at[slots].set(jnp.arange(slots.shape[0], dtype=slots.dtype))
    placed = jnp.take(near, tile_of, axis=0, mode="clip").reshape(count, per_pair, block_len)
    hub_terms = jnp.einsum("bfd,bhsd->hfs", upstream, hub_tiles, preferred_element_type=F32)
    hub_terms = hub_terms.astype(BF).reshape(count, -1, block_len)
    weight_sum = weight_sum.astype(BF).reshape(count, -1, block_len)
    back = swap(jnp.concatenate([placed, hub_terms, weight_sum], axis=1))

    act = act.reshape(feats, hid, share)
    acts = [act[0]] + [trade(act[k], k) for k in range(1, feats)]
    activation = jnp.take(jnp.stack(acts, axis=1), row ^ steps, axis=1, mode="clip")
    activation = activation.reshape(hid, blk_count * block_len)

    sums = jnp.sum(back[:, per_pair : per_pair + hub_rows + 1].astype(F32), axis=0)
    sums = spread(sums.astype(BF))
    returned = back[:, :per_pair].reshape(-1, quarter, block_len)
    own = jnp.einsum("bfd,bsd->bfs", upstream, self_tiles, preferred_element_type=F32)
    send_select = (sends[:, None] == ids[None, :]).astype(BF)
    own = own + jnp.einsum("rfs,rb->bfs", returned, send_select, preferred_element_type=F32)
    own = own.transpose(1, 0, 2).reshape(quarter, blk_count * block_len)
    input_grad, weight_grad = finish(hubs_here, own, sums, quarter, hid, block_len)
    return (activation, weight_grad.T, input_grad)


def solution(mesh):
    return jax.shard_map(
        per_device,
        mesh=mesh,
        in_specs=(
            P("feat", "nodes"),
            P(None, "feat"),
            P("feat", "nodes"),
            P("nodes", None, None),
            P("nodes", None, None, None),
            P("nodes", None, None, None),
            P(),
            P("nodes", None, None),
            P("nodes", None),
        ),
        out_specs=(P("feat", "nodes"), P(None, "feat"), P("feat", "nodes")),
        check_vma=False,
    )
```

```python
import jax
import jax.numpy as jnp
from jax import lax
from jax.experimental import pallas as pl
from jax.experimental.pallas import tpu as pltpu
from jax.sharding import PartitionSpec as P

BF = jnp.bfloat16
F32 = jnp.float32


def silu_slope(pre):
    sig = jax.nn.sigmoid(pre)
    return sig * (1.0 + pre * (1.0 - sig))


def swap(values):
    return lax.all_to_all(values, "nodes", split_axis=0, concat_axis=0, tiled=True)


def trade(values, step):
    count = lax.axis_size("feat")
    return lax.ppermute(values, "feat", [(i, i ^ step) for i in range(count)])


def spread(piece, axes):
    count = 1
    for name in axes:
        count = count * lax.axis_size(name)
    pieces = jnp.broadcast_to(piece[None], (count,) + piece.shape)
    return lax.all_to_all(pieces, axes, split_axis=0, concat_axis=0, tiled=True)


TAIL = 8
SMEM = pl.BlockSpec(memory_space=pltpu.SMEM)
VMEM = pl.BlockSpec(memory_space=pltpu.VMEM)


def pack_kernel(numbers_ref, x_ref, msg_ref, tail_ref):
    quarter = x_ref.shape[0]
    count, rows, block_len = msg_ref.shape
    blk_count = x_ref.shape[1] // block_len
    per_dev = (rows - TAIL) // quarter
    hubs = numbers_ref.shape[0] - count * per_dev
    share = hubs * quarter // count

    def columns(block):
        return pl.ds(pl.multiple_of(block * block_len, block_len), block_len)

    def one(r, carry):
        for k in range(per_dev):
            block = numbers_ref[r * per_dev + k]
            msg_ref[r, k * quarter : (k + 1) * quarter, :] = x_ref[:, columns(block)]
        return carry

    lax.fori_loop(0, count, one, 0, unroll=8)
    tail_ref[...] = jnp.zeros_like(tail_ref)
    for h in range(hubs):
        local = numbers_ref[count * per_dev + h]
        inside = (local >= 0) & (local < blk_count)
        values = x_ref[:, columns(jnp.clip(local, 0, blk_count - 1))].astype(F32)
        values = jnp.where(inside, values, 0.0)
        for i in range(quarter // share):
            place = h * (quarter // share) + i
            tail_ref[place, :share, :] = values[i * share : (i + 1) * share]
    msg_ref[:, per_dev * quarter :, :] = tail_ref[...].astype(BF)


def pack(numbers, x_t, count, per_dev, block_len):
    rows = per_dev * x_t.shape[0] + TAIL
    return pl.pallas_call(
        pack_kernel,
        out_shape=jax.ShapeDtypeStruct((count, rows, block_len), BF),
        in_specs=[SMEM, VMEM],
        out_specs=VMEM,
        scratch_shapes=[pltpu.VMEM((count, TAIL, block_len), F32)],
        compiler_params=pltpu.CompilerParams(vmem_limit_bytes=48 << 20),
        name="pack",
    )(numbers, x_t)


def middle_kernel(row_ref, hub_ref, p0, p1, p2, p3, weight_ref, cot_ref, act_ref, out_ref):
    parts = (p0, p1, p2, p3)
    blks, quarter, block_len = p0.shape
    hid = weight_ref.shape[0] // len(parts)
    weight = weight_ref[...]
    total = jnp.zeros((weight.shape[0], weight.shape[1]), F32)
    for b in range(blks):
        columns = slice(b * block_len, (b + 1) * block_len)
        agg = []
        for k, part in enumerate(parts):
            first = pl.multiple_of((row_ref[0] ^ k) * quarter, quarter)
            agg.append(part[b].astype(F32) + hub_ref[b, pl.ds(first, quarter), :])
        agg = jnp.concatenate(agg, axis=0).astype(BF)
        pre = jnp.dot(weight, agg, preferred_element_type=F32)
        sig = jax.nn.sigmoid(pre)
        act_ref[:, columns] = (pre * sig).astype(BF)
        slope = sig * (1.0 + pre * (1.0 - sig))
        pre_grad = (cot_ref[:, columns].astype(F32) * slope).astype(BF)
        agg_grad = lax.dot_general(
            weight, pre_grad, (((0,), (0,)), ((), ())), preferred_element_type=F32
        ).astype(BF)
        for k in range(len(parts)):
            out_ref[k, b * quarter : (b + 1) * quarter, :] = agg_grad[k * quarter : (k + 1) * quarter]
        total = total + lax.dot_general(
            pre_grad, agg, (((1,), (1,)), ((), ())), preferred_element_type=F32
        )
    total = total.astype(BF)
    for k in range(len(parts)):
        out_ref[k, blks * quarter :, :] = total[k * hid : (k + 1) * hid]


def middle(row, hub_agg, parts, weight, cot):
    blks, quarter, block_len = parts[0].shape
    hid = weight.shape[0] // len(parts)
    return pl.pallas_call(
        middle_kernel,
        out_shape=[
            jax.ShapeDtypeStruct(cot.shape, BF),
            jax.ShapeDtypeStruct((len(parts), blks * quarter + hid, block_len), BF),
        ],
        in_specs=[SMEM] + [VMEM] * (3 + len(parts)),
        out_specs=[VMEM, VMEM],
        compiler_params=pltpu.CompilerParams(vmem_limit_bytes=16 << 20),
        cost_estimate=pl.CostEstimate(flops=6 * weight.size * cot.shape[1], transcendentals=cot.size, bytes_accessed=2 << 20),
        name="middle",
    )(row, hub_agg, *parts, weight, cot)


def finish_kernel(hubs_ref, own_ref, sums_ref, grad_ref, weight_ref, hub_ref):
    quarter = own_ref.shape[0]
    hubs, block_len = hub_ref.shape[0], hub_ref.shape[2]
    blk_count = own_ref.shape[1] // block_len
    count = sums_ref.shape[0]
    share = hubs * quarter // count
    for place in range(count):
        h, i = divmod(place, quarter // share)
        piece = sums_ref[place].astype(F32)
        hub_ref[h, i * share : (i + 1) * share, :] = piece[:share]
        weight_ref[place : place + 1, :] = piece[share : share + 1]
    grad_ref[...] = own_ref[...]
    for h in range(hubs):
        local = hubs_ref[h]

        @pl.when((local >= 0) & (local < blk_count))
        def _():
            first = jnp.clip(local, 0, blk_count - 1) * block_len
            columns = pl.ds(pl.multiple_of(first, block_len), block_len)
            grad_ref[:, columns] += hub_ref[h]


def finish(hubs_here, own, sums, quarter, hid, block_len):
    return pl.pallas_call(
        finish_kernel,
        out_shape=[
            jax.ShapeDtypeStruct(own.shape, F32),
            jax.ShapeDtypeStruct((hid, block_len), F32),
        ],
        in_specs=[SMEM, VMEM, VMEM],
        out_specs=[VMEM, VMEM],
        scratch_shapes=[pltpu.VMEM((hubs_here.shape[0], quarter, block_len), F32)],
        compiler_params=pltpu.CompilerParams(vmem_limit_bytes=16 << 20),
        name="finish",
    )(hubs_here, own, sums)


def per_device(
    x_t, weight, cotangent, self_tiles, hub_tiles, nbr_tiles, hub_ids, send_list, nbr_slot
):
    quarter = x_t.shape[0]
    blk_count, block_len = self_tiles.shape[0], self_tiles.shape[1]
    hubs, nbrs = hub_tiles.shape[1], nbr_tiles.shape[1]
    hid = weight.shape[1]
    count = lax.axis_size("nodes")
    feats = lax.axis_size("feat")
    row = lax.axis_index("feat")
    me = lax.axis_index("nodes")
    sends = send_list[0].reshape(-1)
    slots = nbr_slot[0]
    per_pair = 2 * quarter
    blk_share = blk_count // feats
    share = blk_share * block_len
    steps = jnp.arange(feats, dtype=jnp.int32)

    ids = jnp.arange(blk_count, dtype=jnp.int32)
    hubs_here = hub_ids - me * blk_count
    per_dev = send_list.shape[2]
    got = swap(pack(jnp.concatenate([sends, hubs_here]), x_t, count, per_dev, block_len))

    cot = cotangent.reshape(hid, feats, share)
    cot_parts, weight_parts = [], []
    for k in range(feats):
        part = lax.dynamic_index_in_dim(cot, row ^ k, 1, keepdims=False)
        part = jnp.concatenate([part, weight.T], axis=1)
        part = trade(part, k) if k else part
        cot_parts.append(part[:, :share])
        weight_parts.append(part[:, share:])
    cot_share = jnp.concatenate(cot_parts, axis=0)
    turned = jnp.concatenate(weight_parts, axis=0).reshape(feats * hid, feats, quarter)
    turned = jnp.take(turned, row ^ steps, axis=1, mode="clip")
    feat_ids = jnp.arange(feats * quarter, dtype=jnp.int32)
    owner = row ^ steps[:, None] ^ (feat_ids[None, :] // quarter)
    source = feat_ids[None, :] % quarter + owner * quarter
    unturn = (source[:, None, :] == feat_ids[None, :, None]).astype(BF)

    got, slots, sends, x_t, hubs_here, turned, cot_share, unturn = lax.optimization_barrier(
        (got, slots, sends, x_t, hubs_here, turned, cot_share, unturn)
    )
    blocks = x_t.reshape(quarter, blk_count, block_len).transpose(1, 0, 2)
    hub_rows = hubs * quarter // count
    hub_piece = jnp.sum(got[:, per_pair : per_pair + hub_rows].astype(F32), axis=0).astype(BF)
    hub_x = spread(hub_piece, ("nodes", "feat")).reshape(count, feats, hub_rows, block_len)
    hub_x = hub_x.transpose(1, 0, 2, 3).reshape(feats, hubs, quarter, block_len)

    slot_x = got[:, :per_pair].reshape(-1, quarter, block_len)
    chosen = jnp.take(slot_x, slots, axis=0, mode="clip")
    chosen = chosen.reshape(blk_count, nbrs, quarter, block_len)
    total = jnp.einsum("bjfs,bjsd->bfd", chosen, nbr_tiles, preferred_element_type=F32)
    total = total + jnp.einsum("bfs,bsd->bfd", blocks, self_tiles, preferred_element_type=F32)
    total = total.astype(BF).reshape(feats, blk_share, quarter, block_len)
    parts = []
    for k in range(feats):
        part = lax.dynamic_index_in_dim(total, row ^ k, 0, keepdims=False)
        parts.append(trade(part, k) if k else part)
    hub_share = lax.dynamic_slice_in_dim(hub_tiles, row * blk_share, blk_share, axis=0)
    hub_agg = jnp.einsum("ghfs,bhsd->bgfd", hub_x, hub_share, preferred_element_type=F32)
    hub_agg = hub_agg.reshape(blk_share, feats * quarter, block_len)
    act, message = middle(row.reshape(1), hub_agg, parts, turned.reshape(feats * hid, feats * quarter), cot_share)
    message = jnp.stack([message[0]] + [trade(message[k], k) for k in range(1, feats)])
    upstream = message[:, : blk_share * quarter].reshape(feats, blk_share, quarter, block_len)
    upstream = jnp.take(upstream, row ^ steps, axis=0, mode="clip")
    upstream = upstream.reshape(blk_count, quarter, block_len)
    weight_sum = jnp.einsum(
        "khe,kef->hf", message[:, blk_share * quarter :], unturn, preferred_element_type=F32
    )

    near = jnp.einsum("bfd,bjsd->bjfs", upstream, nbr_tiles, preferred_element_type=F32)
    near = near.astype(BF).reshape(blk_count * nbrs, quarter, block_len)
    tile_of = jnp.zeros_like(slots).at[slots].set(jnp.arange(slots.shape[0], dtype=slots.dtype))
    placed = jnp.take(near, tile_of, axis=0, mode="clip").reshape(count, per_pair, block_len)
    hub_terms = jnp.einsum("bfd,bhsd->hfs", upstream, hub_tiles, preferred_element_type=F32)
    hub_terms = hub_terms.astype(BF).reshape(count, -1, block_len)
    weight_sum = weight_sum.astype(BF).reshape(count, -1, block_len)
    back = swap(jnp.concatenate([placed, hub_terms, weight_sum], axis=1))

    act = act.reshape(feats, hid, share)
    acts = [act[0]] + [trade(act[k], k) for k in range(1, feats)]
    activation = jnp.take(jnp.stack(acts, axis=1), row ^ steps, axis=1, mode="clip")
    activation = activation.reshape(hid, blk_count * block_len)

    sums = jnp.sum(back[:, per_pair : per_pair + hub_rows + 1].astype(F32), axis=0)
    sums = spread(sums.astype(BF), ("nodes",))
    returned = back[:, :per_pair].reshape(-1, quarter, block_len)
    own = jnp.einsum("bfd,bsd->bfs", upstream, self_tiles, preferred_element_type=F32)
    send_select = (sends[:, None] == ids[None, :]).astype(BF)
    own = own + jnp.einsum("rfs,rb->bfs", returned, send_select, preferred_element_type=F32)
    own = own.transpose(1, 0, 2).reshape(quarter, blk_count * block_len)
    input_grad, weight_grad = finish(hubs_here, own, sums, quarter, hid, block_len)
    return (activation, weight_grad.T, input_grad)


def solution(mesh):
    return jax.shard_map(
        per_device,
        mesh=mesh,
        in_specs=(
            P("feat", "nodes"),
            P(None, "feat"),
            P("feat", "nodes"),
            P("nodes", None, None),
            P("nodes", None, None, None),
            P("nodes", None, None, None),
            P(),
            P("nodes", None, None),
            P("nodes", None),
        ),
        out_specs=(P("feat", "nodes"), P(None, "feat"), P("feat", "nodes")),
        check_vma=False,
    )
```

```python
import jax
import jax.numpy as jnp
from jax import lax
from jax.experimental import pallas as pl
from jax.experimental.pallas import tpu as pltpu
from jax.sharding import PartitionSpec as P

BF = jnp.bfloat16
F32 = jnp.float32


def silu_slope(pre):
    sig = jax.nn.sigmoid(pre)
    return sig * (1.0 + pre * (1.0 - sig))


def swap(values):
    return lax.all_to_all(values, "nodes", split_axis=0, concat_axis=0, tiled=True)


def trade(values, step):
    count = lax.axis_size("feat")
    return lax.ppermute(values, "feat", [(i, i ^ step) for i in range(count)])


def spread(piece, axes):
    count = 1
    for name in axes:
        count = count * lax.axis_size(name)
    pieces = jnp.broadcast_to(piece[None], (count,) + piece.shape)
    return lax.all_to_all(pieces, axes, split_axis=0, concat_axis=0, tiled=True)


TAIL = 8
SMEM = pl.BlockSpec(memory_space=pltpu.SMEM)
VMEM = pl.BlockSpec(memory_space=pltpu.VMEM)


def pack_kernel(sends_ref, hubs_ref, x_hbm, msg_ref, x_ref, tail_ref, sem):
    load = pltpu.make_async_copy(x_hbm, x_ref, sem)
    load.start()
    me = lax.axis_index("nodes")
    quarter = x_ref.shape[0]
    count, rows, block_len = msg_ref.shape
    blk_count = x_ref.shape[1] // block_len
    per_dev = (rows - TAIL) // quarter
    hubs = hubs_ref.shape[0]
    share = hubs * quarter // count

    def columns(block):
        return pl.ds(pl.multiple_of(block * block_len, block_len), block_len)

    def one(r, carry):
        for k in range(per_dev):
            block = sends_ref[k, r]
            msg_ref[r, k * quarter : (k + 1) * quarter, :] = x_ref[:, columns(block)]
        return carry

    tail_ref[...] = jnp.zeros_like(tail_ref)
    load.wait()
    lax.fori_loop(0, count, one, 0, unroll=8)
    for h in range(hubs):
        local = hubs_ref[h] - me * blk_count
        inside = (local >= 0) & (local < blk_count)
        values = x_ref[:, columns(jnp.clip(local, 0, blk_count - 1))].astype(F32)
        values = jnp.where(inside, values, 0.0)
        for i in range(quarter // share):
            place = h * (quarter // share) + i
            tail_ref[place, :share, :] = values[i * share : (i + 1) * share]
    msg_ref[:, per_dev * quarter :, :] = tail_ref[...].astype(BF)


def pack(sends, hub_ids, x_t, count, per_dev, block_len):
    rows = per_dev * x_t.shape[0] + TAIL
    return pl.pallas_call(
        pack_kernel,
        out_shape=jax.ShapeDtypeStruct((count, rows, block_len), BF),
        in_specs=[SMEM, SMEM, pl.BlockSpec(memory_space=pl.ANY)],
        out_specs=VMEM,
        scratch_shapes=[
            pltpu.VMEM(x_t.shape, x_t.dtype),
            pltpu.VMEM((count, TAIL, block_len), F32),
            pltpu.SemaphoreType.DMA,
        ],
        compiler_params=pltpu.CompilerParams(vmem_limit_bytes=56 << 20),
        name="pack",
    )(sends, hub_ids, x_t)


def middle_kernel(row_ref, hub_ref, p0, p1, p2, p3, weight_ref, cot_ref, act_ref, out_ref):
    parts = (p0, p1, p2, p3)
    blks, quarter, block_len = p0.shape
    hid = weight_ref.shape[0] // len(parts)
    weight = weight_ref[...]
    total = jnp.zeros((weight.shape[0], weight.shape[1]), F32)
    for b in range(blks):
        columns = slice(b * block_len, (b + 1) * block_len)
        agg = []
        for k, part in enumerate(parts):
            first = pl.multiple_of((row_ref[0] ^ k) * quarter, quarter)
            agg.append(part[b].astype(F32) + hub_ref[b, pl.ds(first, quarter), :])
        agg = jnp.concatenate(agg, axis=0).astype(BF)
        pre = jnp.dot(weight, agg, preferred_element_type=F32)
        sig = jax.nn.sigmoid(pre)
        act_ref[:, columns] = (pre * sig).astype(BF)
        slope = sig * (1.0 + pre * (1.0 - sig))
        pre_grad = (cot_ref[:, columns].astype(F32) * slope).astype(BF)
        agg_grad = lax.dot_general(
            weight, pre_grad, (((0,), (0,)), ((), ())), preferred_element_type=F32
        ).astype(BF)
        for k in range(len(parts)):
            out_ref[k, b * quarter : (b + 1) * quarter, :] = agg_grad[k * quarter : (k + 1) * quarter]
        total = total + lax.dot_general(
            pre_grad, agg, (((1,), (1,)), ((), ())), preferred_element_type=F32
        )
    total = total.astype(BF)
    for k in range(len(parts)):
        out_ref[k, blks * quarter :, :] = total[k * hid : (k + 1) * hid]


def middle(row, hub_agg, parts, weight, cot):
    blks, quarter, block_len = parts[0].shape
    hid = weight.shape[0] // len(parts)
    return pl.pallas_call(
        middle_kernel,
        out_shape=[
            jax.ShapeDtypeStruct(cot.shape, BF),
            jax.ShapeDtypeStruct((len(parts), blks * quarter + hid, block_len), BF),
        ],
        in_specs=[SMEM] + [VMEM] * (3 + len(parts)),
        out_specs=[VMEM, VMEM],
        compiler_params=pltpu.CompilerParams(vmem_limit_bytes=16 << 20),
        cost_estimate=pl.CostEstimate(flops=6 * weight.size * cot.shape[1], transcendentals=cot.size, bytes_accessed=2 << 20),
        name="middle",
    )(row, hub_agg, *parts, weight, cot)


def finish_kernel(hubs_ref, own_ref, sums_ref, grad_ref, weight_ref, hub_ref):
    quarter = own_ref.shape[0]
    hubs, block_len = hub_ref.shape[0], hub_ref.shape[2]
    blk_count = own_ref.shape[1] // block_len
    count = sums_ref.shape[0]
    share = hubs * quarter // count
    for place in range(count):
        h, i = divmod(place, quarter // share)
        piece = sums_ref[place].astype(F32)
        hub_ref[h, i * share : (i + 1) * share, :] = piece[:share]
        weight_ref[place : place + 1, :] = piece[share : share + 1]
    grad_ref[...] = own_ref[...]
    for h in range(hubs):
        local = hubs_ref[h]

        @pl.when((local >= 0) & (local < blk_count))
        def _():
            first = jnp.clip(local, 0, blk_count - 1) * block_len
            columns = pl.ds(pl.multiple_of(first, block_len), block_len)
            grad_ref[:, columns] += hub_ref[h]


def finish(hubs_here, own, sums, quarter, hid, block_len):
    return pl.pallas_call(
        finish_kernel,
        out_shape=[
            jax.ShapeDtypeStruct(own.shape, F32),
            jax.ShapeDtypeStruct((hid, block_len), F32),
        ],
        in_specs=[SMEM, VMEM, VMEM],
        out_specs=[VMEM, VMEM],
        scratch_shapes=[pltpu.VMEM((hubs_here.shape[0], quarter, block_len), F32)],
        compiler_params=pltpu.CompilerParams(vmem_limit_bytes=16 << 20),
        name="finish",
    )(hubs_here, own, sums)


def per_device(
    x_t, weight, cotangent, self_tiles, hub_tiles, nbr_tiles, hub_ids, send_list, nbr_slot
):
    quarter = x_t.shape[0]
    blk_count, block_len = self_tiles.shape[0], self_tiles.shape[1]
    hubs, nbrs = hub_tiles.shape[1], nbr_tiles.shape[1]
    hid = weight.shape[1]
    count = lax.axis_size("nodes")
    feats = lax.axis_size("feat")
    row = lax.axis_index("feat")
    me = lax.axis_index("nodes")
    sends = send_list[0].reshape(-1)
    slots = nbr_slot[0]
    per_pair = 2 * quarter
    blk_share = blk_count // feats
    share = blk_share * block_len
    steps = jnp.arange(feats, dtype=jnp.int32)

    ids = jnp.arange(blk_count, dtype=jnp.int32)
    hubs_here = hub_ids - me * blk_count
    per_dev = send_list.shape[2]
    got = swap(pack(send_list[0].T, hub_ids, x_t, count, per_dev, block_len))

    cot = cotangent.reshape(hid, feats, share)
    cot_parts, weight_parts = [], []
    for k in range(feats):
        part = lax.dynamic_index_in_dim(cot, row ^ k, 1, keepdims=False)
        part = jnp.concatenate([part, weight.T], axis=1)
        part = trade(part, k) if k else part
        cot_parts.append(part[:, :share])
        weight_parts.append(part[:, share:])
    cot_share = jnp.concatenate(cot_parts, axis=0)
    turned = jnp.concatenate(weight_parts, axis=0).reshape(feats * hid, feats, quarter)
    turned = jnp.take(turned, row ^ steps, axis=1, mode="clip")
    feat_ids = jnp.arange(feats * quarter, dtype=jnp.int32)
    owner = row ^ steps[:, None] ^ (feat_ids[None, :] // quarter)
    source = feat_ids[None, :] % quarter + owner * quarter
    unturn = (source[:, None, :] == feat_ids[None, :, None]).astype(BF)

    got, slots, sends, x_t, hubs_here, turned, cot_share, unturn = lax.optimization_barrier(
        (got, slots, sends, x_t, hubs_here, turned, cot_share, unturn)
    )
    blocks = x_t.reshape(quarter, blk_count, block_len).transpose(1, 0, 2)
    hub_rows = hubs * quarter // count
    hub_piece = jnp.sum(got[:, per_pair : per_pair + hub_rows].astype(F32), axis=0).astype(BF)
    hub_x = spread(hub_piece, ("nodes", "feat")).reshape(count, feats, hub_rows, block_len)
    hub_x = hub_x.transpose(1, 0, 2, 3).reshape(feats, hubs, quarter, block_len)

    slot_x = got[:, :per_pair].reshape(-1, quarter, block_len)
    chosen = jnp.take(slot_x, slots, axis=0, mode="clip")
    chosen = chosen.reshape(blk_count, nbrs, quarter, block_len)
    total = jnp.einsum("bjfs,bjsd->bfd", chosen, nbr_tiles, preferred_element_type=F32)
    total = total + jnp.einsum("bfs,bsd->bfd", blocks, self_tiles, preferred_element_type=F32)
    total = total.astype(BF).reshape(feats, blk_share, quarter, block_len)
    parts = []
    for k in range(feats):
        part = lax.dynamic_index_in_dim(total, row ^ k, 0, keepdims=False)
        parts.append(trade(part, k) if k else part)
    hub_share = lax.dynamic_slice_in_dim(hub_tiles, row * blk_share, blk_share, axis=0)
    hub_agg = jnp.einsum("ghfs,bhsd->bgfd", hub_x, hub_share, preferred_element_type=F32)
    hub_agg = hub_agg.reshape(blk_share, feats * quarter, block_len)
    act, message = middle(row.reshape(1), hub_agg, parts, turned.reshape(feats * hid, feats * quarter), cot_share)
    message = jnp.stack([message[0]] + [trade(message[k], k) for k in range(1, feats)])
    upstream = message[:, : blk_share * quarter].reshape(feats, blk_share, quarter, block_len)
    upstream = jnp.take(upstream, row ^ steps, axis=0, mode="clip")
    upstream = upstream.reshape(blk_count, quarter, block_len)
    weight_sum = jnp.einsum(
        "khe,kef->hf", message[:, blk_share * quarter :], unturn, preferred_element_type=F32
    )

    near = jnp.einsum("bfd,bjsd->bjfs", upstream, nbr_tiles, preferred_element_type=F32)
    near = near.astype(BF).reshape(blk_count * nbrs, quarter, block_len)
    tile_of = jnp.zeros_like(slots).at[slots].set(jnp.arange(slots.shape[0], dtype=slots.dtype))
    placed = jnp.take(near, tile_of, axis=0, mode="clip").reshape(count, per_pair, block_len)
    hub_terms = jnp.einsum("bfd,bhsd->hfs", upstream, hub_tiles, preferred_element_type=F32)
    hub_terms = hub_terms.astype(BF).reshape(count, -1, block_len)
    weight_sum = weight_sum.astype(BF).reshape(count, -1, block_len)
    back = swap(jnp.concatenate([placed, hub_terms, weight_sum], axis=1))

    act = act.reshape(feats, hid, share)
    acts = [act[0]] + [trade(act[k], k) for k in range(1, feats)]
    activation = jnp.take(jnp.stack(acts, axis=1), row ^ steps, axis=1, mode="clip")
    activation = activation.reshape(hid, blk_count * block_len)

    sums = jnp.sum(back[:, per_pair : per_pair + hub_rows + 1].astype(F32), axis=0)
    sums = spread(sums.astype(BF), ("nodes",))
    returned = back[:, :per_pair].reshape(-1, quarter, block_len)
    own = jnp.einsum("bfd,bsd->bfs", upstream, self_tiles, preferred_element_type=F32)
    send_select = (sends[:, None] == ids[None, :]).astype(BF)
    own = own + jnp.einsum("rfs,rb->bfs", returned, send_select, preferred_element_type=F32)
    own = own.transpose(1, 0, 2).reshape(quarter, blk_count * block_len)
    input_grad, weight_grad = finish(hubs_here, own, sums, quarter, hid, block_len)
    return (activation, weight_grad.T, input_grad)


def solution(mesh):
    return jax.shard_map(
        per_device,
        mesh=mesh,
        in_specs=(
            P("feat", "nodes"),
            P(None, "feat"),
            P("feat", "nodes"),
            P("nodes", None, None),
            P("nodes", None, None, None),
            P("nodes", None, None, None),
            P(),
            P("nodes", None, None),
            P("nodes", None),
        ),
        out_specs=(P("feat", "nodes"), P(None, "feat"), P("feat", "nodes")),
        check_vma=False,
    )
```

```python
import jax
import jax.numpy as jnp
from jax import lax
from jax.experimental import pallas as pl
from jax.experimental.pallas import tpu as pltpu
from jax.sharding import PartitionSpec as P

BF = jnp.bfloat16
F32 = jnp.float32


def silu_slope(pre):
    sig = jax.nn.sigmoid(pre)
    return sig * (1.0 + pre * (1.0 - sig))


def swap(values):
    return lax.all_to_all(values, "nodes", split_axis=0, concat_axis=0, tiled=True)


def trade(values, step):
    count = lax.axis_size("feat")
    return lax.ppermute(values, "feat", [(i, i ^ step) for i in range(count)])


def spread(piece, axes):
    count = 1
    for name in axes:
        count = count * lax.axis_size(name)
    pieces = jnp.broadcast_to(piece[None], (count,) + piece.shape)
    return lax.all_to_all(pieces, axes, split_axis=0, concat_axis=0, tiled=True)


TAIL = 8
SMEM = pl.BlockSpec(memory_space=pltpu.SMEM)
VMEM = pl.BlockSpec(memory_space=pltpu.VMEM)


def pack_kernel(sends_ref, hubs_ref, x_hbm, out_hbm, msg_ref, x_ref, tail_ref, sem, out_sems):
    load = pltpu.make_async_copy(x_hbm, x_ref, sem)
    load.start()
    me = lax.axis_index("nodes")
    quarter = x_ref.shape[0]
    count, rows, block_len = msg_ref.shape
    blk_count = x_ref.shape[1] // block_len
    per_dev = (rows - TAIL) // quarter
    hubs = hubs_ref.shape[0]
    share = hubs * quarter // count

    def columns(block):
        return pl.ds(pl.multiple_of(block * block_len, block_len), block_len)

    def one(r, carry):
        for k in range(per_dev):
            block = sends_ref[k, r]
            msg_ref[r, k * quarter : (k + 1) * quarter, :] = x_ref[:, columns(block)]
        return carry

    tail_ref[...] = jnp.zeros_like(tail_ref)
    load.wait()
    for h in range(hubs):
        local = hubs_ref[h] - me * blk_count
        inside = (local >= 0) & (local < blk_count)
        values = x_ref[:, columns(jnp.clip(local, 0, blk_count - 1))].astype(F32)
        values = jnp.where(inside, values, 0.0)
        for i in range(quarter // share):
            place = h * (quarter // share) + i
            tail_ref[place, :share, :] = values[i * share : (i + 1) * share]
    msg_ref[:, per_dev * quarter :, :] = tail_ref[...].astype(BF)
    lots = out_sems.shape[0]
    size = count // lots
    stores = []
    for lot in range(lots):
        lax.fori_loop(lot * size, (lot + 1) * size, one, 0, unroll=8)
        part = pl.ds(lot * size, size)
        stores.append(pltpu.make_async_copy(msg_ref.at[part], out_hbm.at[part], out_sems.at[lot]))
        stores[-1].start()
    for store in stores:
        store.wait()


def pack(sends, hub_ids, x_t, count, per_dev, block_len):
    rows = per_dev * x_t.shape[0] + TAIL
    return pl.pallas_call(
        pack_kernel,
        out_shape=jax.ShapeDtypeStruct((count, rows, block_len), BF),
        in_specs=[SMEM, SMEM, pl.BlockSpec(memory_space=pl.ANY)],
        out_specs=pl.BlockSpec(memory_space=pl.ANY),
        scratch_shapes=[
            pltpu.VMEM((count, rows, block_len), BF),
            pltpu.VMEM(x_t.shape, x_t.dtype),
            pltpu.VMEM((count, TAIL, block_len), F32),
            pltpu.SemaphoreType.DMA,
            pltpu.SemaphoreType.DMA((4,)),
        ],
        compiler_params=pltpu.CompilerParams(vmem_limit_bytes=56 << 20),
        name="pack",
    )(sends, hub_ids, x_t)


def middle_kernel(row_ref, hub_ref, p0, p1, p2, p3, weight_ref, cot_ref, act_ref, out_ref):
    parts = (p0, p1, p2, p3)
    blks, quarter, block_len = p0.shape
    hid = weight_ref.shape[0] // len(parts)
    weight = weight_ref[...]
    total = jnp.zeros((weight.shape[0], weight.shape[1]), F32)
    for b in range(blks):
        columns = slice(b * block_len, (b + 1) * block_len)
        agg = []
        for k, part in enumerate(parts):
            first = pl.multiple_of((row_ref[0] ^ k) * quarter, quarter)
            agg.append(part[b].astype(F32) + hub_ref[b, pl.ds(first, quarter), :])
        agg = jnp.concatenate(agg, axis=0).astype(BF)
        pre = jnp.dot(weight, agg, preferred_element_type=F32)
        sig = jax.nn.sigmoid(pre)
        act_ref[:, columns] = (pre * sig).astype(BF)
        slope = sig * (1.0 + pre * (1.0 - sig))
        pre_grad = (cot_ref[:, columns].astype(F32) * slope).astype(BF)
        agg_grad = lax.dot_general(
            weight, pre_grad, (((0,), (0,)), ((), ())), preferred_element_type=F32
        ).astype(BF)
        for k in range(len(parts)):
            out_ref[k, b * quarter : (b + 1) * quarter, :] = agg_grad[k * quarter : (k + 1) * quarter]
        total = total + lax.dot_general(
            pre_grad, agg, (((1,), (1,)), ((), ())), preferred_element_type=F32
        )
    total = total.astype(BF)
    for k in range(len(parts)):
        out_ref[k, blks * quarter :, :] = total[k * hid : (k + 1) * hid]


def middle(row, hub_agg, parts, weight, cot):
    blks, quarter, block_len = parts[0].shape
    hid = weight.shape[0] // len(parts)
    return pl.pallas_call(
        middle_kernel,
        out_shape=[
            jax.ShapeDtypeStruct(cot.shape, BF),
            jax.ShapeDtypeStruct((len(parts), blks * quarter + hid, block_len), BF),
        ],
        in_specs=[SMEM] + [VMEM] * (3 + len(parts)),
        out_specs=[VMEM, VMEM],
        compiler_params=pltpu.CompilerParams(vmem_limit_bytes=16 << 20),
        cost_estimate=pl.CostEstimate(flops=6 * weight.size * cot.shape[1], transcendentals=cot.size, bytes_accessed=2 << 20),
        name="middle",
    )(row, hub_agg, *parts, weight, cot)


def finish_kernel(hubs_ref, own_ref, sums_ref, grad_ref, weight_ref, hub_ref):
    quarter = own_ref.shape[0]
    hubs, block_len = hub_ref.shape[0], hub_ref.shape[2]
    blk_count = own_ref.shape[1] // block_len
    count = sums_ref.shape[0]
    share = hubs * quarter // count
    for place in range(count):
        h, i = divmod(place, quarter // share)
        piece = sums_ref[place].astype(F32)
        hub_ref[h, i * share : (i + 1) * share, :] = piece[:share]
        weight_ref[place : place + 1, :] = piece[share : share + 1]
    grad_ref[...] = own_ref[...]
    for h in range(hubs):
        local = hubs_ref[h]

        @pl.when((local >= 0) & (local < blk_count))
        def _():
            first = jnp.clip(local, 0, blk_count - 1) * block_len
            columns = pl.ds(pl.multiple_of(first, block_len), block_len)
            grad_ref[:, columns] += hub_ref[h]


def finish(hubs_here, own, sums, quarter, hid, block_len):
    return pl.pallas_call(
        finish_kernel,
        out_shape=[
            jax.ShapeDtypeStruct(own.shape, F32),
            jax.ShapeDtypeStruct((hid, block_len), F32),
        ],
        in_specs=[SMEM, VMEM, VMEM],
        out_specs=[VMEM, VMEM],
        scratch_shapes=[pltpu.VMEM((hubs_here.shape[0], quarter, block_len), F32)],
        compiler_params=pltpu.CompilerParams(vmem_limit_bytes=16 << 20),
        name="finish",
    )(hubs_here, own, sums)


def per_device(
    x_t, weight, cotangent, self_tiles, hub_tiles, nbr_tiles, hub_ids, send_list, nbr_slot
):
    quarter = x_t.shape[0]
    blk_count, block_len = self_tiles.shape[0], self_tiles.shape[1]
    hubs, nbrs = hub_tiles.shape[1], nbr_tiles.shape[1]
    hid = weight.shape[1]
    count = lax.axis_size("nodes")
    feats = lax.axis_size("feat")
    row = lax.axis_index("feat")
    me = lax.axis_index("nodes")
    sends = send_list[0].reshape(-1)
    slots = nbr_slot[0]
    per_pair = 2 * quarter
    blk_share = blk_count // feats
    share = blk_share * block_len
    steps = jnp.arange(feats, dtype=jnp.int32)

    ids = jnp.arange(blk_count, dtype=jnp.int32)
    hubs_here = hub_ids - me * blk_count
    per_dev = send_list.shape[2]
    got = swap(pack(send_list[0].T, hub_ids, x_t, count, per_dev, block_len))

    cot = cotangent.reshape(hid, feats, share)
    cot_parts, weight_parts = [], []
    for k in range(feats):
        part = lax.dynamic_index_in_dim(cot, row ^ k, 1, keepdims=False)
        part = jnp.concatenate([part, weight.T], axis=1)
        part = trade(part, k) if k else part
        cot_parts.append(part[:, :share])
        weight_parts.append(part[:, share:])
    cot_share = jnp.concatenate(cot_parts, axis=0)
    turned = jnp.concatenate(weight_parts, axis=0).reshape(feats * hid, feats, quarter)
    turned = jnp.take(turned, row ^ steps, axis=1, mode="clip")
    feat_ids = jnp.arange(feats * quarter, dtype=jnp.int32)
    owner = row ^ steps[:, None] ^ (feat_ids[None, :] // quarter)
    source = feat_ids[None, :] % quarter + owner * quarter
    unturn = (source[:, None, :] == feat_ids[None, :, None]).astype(BF)

    got, slots, sends, x_t, hubs_here, turned, cot_share, unturn = lax.optimization_barrier(
        (got, slots, sends, x_t, hubs_here, turned, cot_share, unturn)
    )
    blocks = x_t.reshape(quarter, blk_count, block_len).transpose(1, 0, 2)
    hub_rows = hubs * quarter // count
    hub_piece = jnp.sum(got[:, per_pair : per_pair + hub_rows].astype(F32), axis=0).astype(BF)
    hub_x = spread(hub_piece, ("nodes", "feat")).reshape(count, feats, hub_rows, block_len)
    hub_x = hub_x.transpose(1, 0, 2, 3).reshape(feats, hubs, quarter, block_len)

    slot_x = got[:, :per_pair].reshape(-1, quarter, block_len)
    chosen = jnp.take(slot_x, slots, axis=0, mode="clip")
    chosen = chosen.reshape(blk_count, nbrs, quarter, block_len)
    total = jnp.einsum("bjfs,bjsd->bfd", chosen, nbr_tiles, preferred_element_type=F32)
    total = total + jnp.einsum("bfs,bsd->bfd", blocks, self_tiles, preferred_element_type=F32)
    total = total.astype(BF).reshape(feats, blk_share, quarter, block_len)
    parts = []
    for k in range(feats):
        part = lax.dynamic_index_in_dim(total, row ^ k, 0, keepdims=False)
        parts.append(trade(part, k) if k else part)
    hub_share = lax.dynamic_slice_in_dim(hub_tiles, row * blk_share, blk_share, axis=0)
    hub_agg = jnp.einsum("ghfs,bhsd->bgfd", hub_x, hub_share, preferred_element_type=F32)
    hub_agg = hub_agg.reshape(blk_share, feats * quarter, block_len)
    act, message = middle(row.reshape(1), hub_agg, parts, turned.reshape(feats * hid, feats * quarter), cot_share)
    messages = [message[0]] + [trade(message[k], k) for k in range(1, feats)]
    message = jnp.stack(messages)
    upstream = []
    for q in range(feats):
        share_of_q = messages[0][: blk_share * quarter]
        for k in range(1, feats):
            share_of_q = jnp.where(row == q ^ k, messages[k][: blk_share * quarter], share_of_q)
        upstream.append(share_of_q)
    upstream = jnp.concatenate(upstream, axis=0).reshape(blk_count, quarter, block_len)
    weight_sum = jnp.einsum(
        "khe,kef->hf", message[:, blk_share * quarter :], unturn, preferred_element_type=F32
    )

    near = jnp.einsum("bfd,bjsd->bjfs", upstream, nbr_tiles, preferred_element_type=F32)
    near = near.astype(BF).reshape(blk_count * nbrs, quarter, block_len)
    tile_of = jnp.zeros_like(slots).at[slots].set(jnp.arange(slots.shape[0], dtype=slots.dtype))
    placed = jnp.take(near, tile_of, axis=0, mode="clip").reshape(count, per_pair, block_len)
    hub_terms = jnp.einsum("bfd,bhsd->hfs", upstream, hub_tiles, preferred_element_type=F32)
    hub_terms = hub_terms.astype(BF).reshape(count, -1, block_len)
    weight_sum = weight_sum.astype(BF).reshape(count, -1, block_len)
    back = swap(jnp.concatenate([placed, hub_terms, weight_sum], axis=1))

    act = act.reshape(feats, hid, share)
    acts = [act[0]] + [trade(act[k], k) for k in range(1, feats)]
    activation = jnp.take(jnp.stack(acts, axis=1), row ^ steps, axis=1, mode="clip")
    activation = activation.reshape(hid, blk_count * block_len)

    sums = jnp.sum(back[:, per_pair : per_pair + hub_rows + 1].astype(F32), axis=0)
    sums = spread(sums.astype(BF), ("nodes",))
    returned = back[:, :per_pair].reshape(-1, quarter, block_len)
    own = jnp.einsum("bfd,bsd->bfs", upstream, self_tiles, preferred_element_type=F32)
    send_select = (sends[:, None] == ids[None, :]).astype(BF)
    own = own + jnp.einsum("rfs,rb->bfs", returned, send_select, preferred_element_type=F32)
    own = own.transpose(1, 0, 2).reshape(quarter, blk_count * block_len)
    input_grad, weight_grad = finish(hubs_here, own, sums, quarter, hid, block_len)
    return (activation, weight_grad.T, input_grad)


def solution(mesh):
    return jax.shard_map(
        per_device,
        mesh=mesh,
        in_specs=(
            P("feat", "nodes"),
            P(None, "feat"),
            P("feat", "nodes"),
            P("nodes", None, None),
            P("nodes", None, None, None),
            P("nodes", None, None, None),
            P(),
            P("nodes", None, None),
            P("nodes", None),
        ),
        out_specs=(P("feat", "nodes"), P(None, "feat"), P("feat", "nodes")),
        check_vma=False,
    )
```

```python
import jax
import jax.numpy as jnp
from jax import lax
from jax.experimental import pallas as pl
from jax.experimental.pallas import tpu as pltpu
from jax.sharding import PartitionSpec as P

BF = jnp.bfloat16
F32 = jnp.float32


def silu_slope(pre):
    sig = jax.nn.sigmoid(pre)
    return sig * (1.0 + pre * (1.0 - sig))


def swap(values):
    return lax.all_to_all(values, "nodes", split_axis=0, concat_axis=0, tiled=True)


def trade(values, step):
    count = lax.axis_size("feat")
    return lax.ppermute(values, "feat", [(i, i ^ step) for i in range(count)])


def spread(piece, axes):
    count = 1
    for name in axes:
        count = count * lax.axis_size(name)
    pieces = jnp.broadcast_to(piece[None], (count,) + piece.shape)
    return lax.all_to_all(pieces, axes, split_axis=0, concat_axis=0, tiled=True)


TAIL = 8
SMEM = pl.BlockSpec(memory_space=pltpu.SMEM)
VMEM = pl.BlockSpec(memory_space=pltpu.VMEM)


def pack_kernel(sends_ref, hubs_ref, x_hbm, msg_ref, x_ref, tail_ref, sem):
    load = pltpu.make_async_copy(x_hbm, x_ref, sem)
    load.start()
    me = lax.axis_index("nodes")
    quarter = x_ref.shape[0]
    count, rows, block_len = msg_ref.shape
    blk_count = x_ref.shape[1] // block_len
    per_dev = (rows - TAIL) // quarter
    hubs = hubs_ref.shape[0]
    share = hubs * quarter // count

    def columns(block):
        return pl.ds(pl.multiple_of(block * block_len, block_len), block_len)

    def one(r, carry):
        for k in range(per_dev):
            block = sends_ref[k, r]
            msg_ref[r, k * quarter : (k + 1) * quarter, :] = x_ref[:, columns(block)]
        return carry

    tail_ref[...] = jnp.zeros_like(tail_ref)
    load.wait()
    lax.fori_loop(0, count, one, 0, unroll=8)
    for h in range(hubs):
        local = hubs_ref[h] - me * blk_count
        inside = (local >= 0) & (local < blk_count)
        values = x_ref[:, columns(jnp.clip(local, 0, blk_count - 1))].astype(F32)
        values = jnp.where(inside, values, 0.0)
        for i in range(quarter // share):
            place = h * (quarter // share) + i
            tail_ref[place, :share, :] = values[i * share : (i + 1) * share]
    msg_ref[:, per_dev * quarter :, :] = tail_ref[...].astype(BF)


def pack(sends, hub_ids, x_t, count, per_dev, block_len):
    rows = per_dev * x_t.shape[0] + TAIL
    return pl.pallas_call(
        pack_kernel,
        out_shape=jax.ShapeDtypeStruct((count, rows, block_len), BF),
        in_specs=[SMEM, SMEM, pl.BlockSpec(memory_space=pl.ANY)],
        out_specs=VMEM,
        scratch_shapes=[
            pltpu.VMEM(x_t.shape, x_t.dtype),
            pltpu.VMEM((count, TAIL, block_len), F32),
            pltpu.SemaphoreType.DMA,
        ],
        compiler_params=pltpu.CompilerParams(vmem_limit_bytes=56 << 20),
        name="pack",
    )(sends, hub_ids, x_t)


def middle_kernel(row_ref, hub_ref, p0, p1, p2, p3, weight_ref, cot_ref, act_ref, out_ref):
    parts = (p0, p1, p2, p3)
    blks, quarter, block_len = p0.shape
    hid = weight_ref.shape[0] // len(parts)
    weight = weight_ref[...]
    total = jnp.zeros((weight.shape[0], weight.shape[1]), F32)
    for b in range(blks):
        columns = slice(b * block_len, (b + 1) * block_len)
        agg = []
        for k, part in enumerate(parts):
            first = pl.multiple_of((row_ref[0] ^ k) * quarter, quarter)
            agg.append(part[b].astype(F32) + hub_ref[b, pl.ds(first, quarter), :])
        agg = jnp.concatenate(agg, axis=0).astype(BF)
        pre = jnp.dot(weight, agg, preferred_element_type=F32)
        sig = jax.nn.sigmoid(pre)
        act_ref[:, columns] = (pre * sig).astype(BF)
        slope = sig * (1.0 + pre * (1.0 - sig))
        pre_grad = (cot_ref[:, columns].astype(F32) * slope).astype(BF)
        agg_grad = lax.dot_general(
            weight, pre_grad, (((0,), (0,)), ((), ())), preferred_element_type=F32
        ).astype(BF)
        for k in range(len(parts)):
            out_ref[k, b * quarter : (b + 1) * quarter, :] = agg_grad[k * quarter : (k + 1) * quarter]
        total = total + lax.dot_general(
            pre_grad, agg, (((1,), (1,)), ((), ())), preferred_element_type=F32
        )
    total = total.astype(BF)
    for k in range(len(parts)):
        out_ref[k, blks * quarter :, :] = total[k * hid : (k + 1) * hid]


def middle(row, hub_agg, parts, weight, cot):
    blks, quarter, block_len = parts[0].shape
    hid = weight.shape[0] // len(parts)
    return pl.pallas_call(
        middle_kernel,
        out_shape=[
            jax.ShapeDtypeStruct(cot.shape, BF),
            jax.ShapeDtypeStruct((len(parts), blks * quarter + hid, block_len), BF),
        ],
        in_specs=[SMEM] + [VMEM] * (3 + len(parts)),
        out_specs=[VMEM, VMEM],
        compiler_params=pltpu.CompilerParams(vmem_limit_bytes=16 << 20),
        cost_estimate=pl.CostEstimate(flops=6 * weight.size * cot.shape[1], transcendentals=cot.size, bytes_accessed=2 << 20),
        name="middle",
    )(row, hub_agg, *parts, weight, cot)


def finish_kernel(hubs_ref, own_ref, sums_ref, grad_ref, weight_ref, hub_ref):
    quarter = own_ref.shape[0]
    hubs, block_len = hub_ref.shape[0], hub_ref.shape[2]
    blk_count = own_ref.shape[1] // block_len
    count = sums_ref.shape[0]
    share = hubs * quarter // count
    for place in range(count):
        h, i = divmod(place, quarter // share)
        piece = sums_ref[place].astype(F32)
        hub_ref[h, i * share : (i + 1) * share, :] = piece[:share]
        weight_ref[place : place + 1, :] = piece[share : share + 1]
    grad_ref[...] = own_ref[...]
    for h in range(hubs):
        local = hubs_ref[h]

        @pl.when((local >= 0) & (local < blk_count))
        def _():
            first = jnp.clip(local, 0, blk_count - 1) * block_len
            columns = pl.ds(pl.multiple_of(first, block_len), block_len)
            grad_ref[:, columns] += hub_ref[h]


def finish(hubs_here, own, sums, quarter, hid, block_len):
    return pl.pallas_call(
        finish_kernel,
        out_shape=[
            jax.ShapeDtypeStruct(own.shape, F32),
            jax.ShapeDtypeStruct((hid, block_len), F32),
        ],
        in_specs=[SMEM, VMEM, VMEM],
        out_specs=[VMEM, VMEM],
        scratch_shapes=[pltpu.VMEM((hubs_here.shape[0], quarter, block_len), F32)],
        compiler_params=pltpu.CompilerParams(vmem_limit_bytes=16 << 20),
        name="finish",
    )(hubs_here, own, sums)


def per_device(
    x_t, weight, cotangent, self_tiles, hub_tiles, nbr_tiles, hub_ids, send_list, nbr_slot
):
    quarter = x_t.shape[0]
    blk_count, block_len = self_tiles.shape[0], self_tiles.shape[1]
    hubs, nbrs = hub_tiles.shape[1], nbr_tiles.shape[1]
    hid = weight.shape[1]
    count = lax.axis_size("nodes")
    feats = lax.axis_size("feat")
    row = lax.axis_index("feat")
    me = lax.axis_index("nodes")
    sends = send_list[0].reshape(-1)
    slots = nbr_slot[0]
    per_pair = 2 * quarter
    blk_share = blk_count // feats
    share = blk_share * block_len
    steps = jnp.arange(feats, dtype=jnp.int32)

    ids = jnp.arange(blk_count, dtype=jnp.int32)
    hubs_here = hub_ids - me * blk_count
    per_dev = send_list.shape[2]
    got = swap(pack(send_list[0].T, hub_ids, x_t, count, per_dev, block_len))

    cot = cotangent.reshape(hid, feats, share)
    cot_parts, weight_parts = [], []
    for k in range(feats):
        part = lax.dynamic_index_in_dim(cot, row ^ k, 1, keepdims=False)
        part = jnp.concatenate([part, weight.T], axis=1)
        part = trade(part, k) if k else part
        cot_parts.append(part[:, :share])
        weight_parts.append(part[:, share:])
    cot_share = jnp.concatenate(cot_parts, axis=0)
    turned = jnp.concatenate(weight_parts, axis=0).reshape(feats * hid, feats, quarter)
    turned = jnp.take(turned, row ^ steps, axis=1, mode="clip")
    feat_ids = jnp.arange(feats * quarter, dtype=jnp.int32)
    owner = row ^ steps[:, None] ^ (feat_ids[None, :] // quarter)
    source = feat_ids[None, :] % quarter + owner * quarter
    unturn = (source[:, None, :] == feat_ids[None, :, None]).astype(BF)

    got, slots, sends, x_t, hubs_here, turned, cot_share, unturn = lax.optimization_barrier(
        (got, slots, sends, x_t, hubs_here, turned, cot_share, unturn)
    )
    blocks = x_t.reshape(quarter, blk_count, block_len).transpose(1, 0, 2)
    hub_rows = hubs * quarter // count
    hub_piece = jnp.sum(got[:, per_pair : per_pair + hub_rows].astype(F32), axis=0).astype(BF)
    hub_x = spread(hub_piece, ("nodes", "feat")).reshape(count, feats, hub_rows, block_len)
    hub_x = hub_x.transpose(1, 0, 2, 3).reshape(feats, hubs, quarter, block_len)

    slot_x = got[:, :per_pair].reshape(-1, quarter, block_len)
    chosen = jnp.take(slot_x, slots, axis=0, mode="clip")
    chosen = chosen.reshape(blk_count, nbrs, quarter, block_len)
    total = jnp.einsum("bjfs,bjsd->bfd", chosen, nbr_tiles, preferred_element_type=F32)
    total = total + jnp.einsum("bfs,bsd->bfd", blocks, self_tiles, preferred_element_type=F32)
    total = total.astype(BF).reshape(feats, blk_share, quarter, block_len)
    parts = []
    for k in range(feats):
        part = lax.dynamic_index_in_dim(total, row ^ k, 0, keepdims=False)
        parts.append(trade(part, k) if k else part)
    hub_share = lax.dynamic_slice_in_dim(hub_tiles, row * blk_share, blk_share, axis=0)
    hub_agg = jnp.einsum("ghfs,bhsd->bgfd", hub_x, hub_share, preferred_element_type=F32)
    hub_agg = hub_agg.reshape(blk_share, feats * quarter, block_len)
    act, message = middle(row.reshape(1), hub_agg, parts, turned.reshape(feats * hid, feats * quarter), cot_share)
    messages = [message[0]] + [trade(message[k], k) for k in range(1, feats)]
    message = jnp.stack(messages)
    upstream = []
    for q in range(feats):
        share_of_q = messages[0][: blk_share * quarter]
        for k in range(1, feats):
            share_of_q = jnp.where(row == q ^ k, messages[k][: blk_share * quarter], share_of_q)
        upstream.append(share_of_q)
    upstream = jnp.concatenate(upstream, axis=0).reshape(blk_count, quarter, block_len)
    weight_sum = jnp.einsum(
        "khe,kef->hf", message[:, blk_share * quarter :], unturn, preferred_element_type=F32
    )

    near = jnp.einsum("bfd,bjsd->bjfs", upstream, nbr_tiles, preferred_element_type=F32)
    near = near.astype(BF).reshape(blk_count * nbrs, quarter, block_len)
    tile_of = jnp.zeros_like(slots).at[slots].set(jnp.arange(slots.shape[0], dtype=slots.dtype))
    placed = jnp.take(near, tile_of, axis=0, mode="clip").reshape(count, per_pair, block_len)
    hub_terms = jnp.einsum("bfd,bhsd->hfs", upstream, hub_tiles, preferred_element_type=F32)
    hub_terms = hub_terms.astype(BF).reshape(count, -1, block_len)
    weight_sum = weight_sum.astype(BF).reshape(count, -1, block_len)
    back = swap(jnp.concatenate([placed, hub_terms, weight_sum], axis=1))

    act = act.reshape(feats, hid, share)
    acts = [act[0]] + [trade(act[k], k) for k in range(1, feats)]
    activation = jnp.take(jnp.stack(acts, axis=1), row ^ steps, axis=1, mode="clip")
    activation = activation.reshape(hid, blk_count * block_len)

    sums = jnp.sum(back[:, per_pair : per_pair + hub_rows + 1].astype(F32), axis=0)
    sums = spread(sums.astype(BF), ("nodes",))
    returned = back[:, :per_pair].reshape(-1, quarter, block_len)
    own = jnp.einsum("bfd,bsd->bfs", upstream, self_tiles, preferred_element_type=F32)
    send_select = (sends[:, None] == ids[None, :]).astype(BF)
    own = own + jnp.einsum("rfs,rb->bfs", returned, send_select, preferred_element_type=F32)
    own = own.transpose(1, 0, 2).reshape(quarter, blk_count * block_len)
    input_grad, weight_grad = finish(hubs_here, own, sums, quarter, hid, block_len)
    return (activation, weight_grad.T, input_grad)


def solution(mesh):
    return jax.shard_map(
        per_device,
        mesh=mesh,
        in_specs=(
            P("feat", "nodes"),
            P(None, "feat"),
            P("feat", "nodes"),
            P("nodes", None, None),
            P("nodes", None, None, None),
            P("nodes", None, None, None),
            P(),
            P("nodes", None, None),
            P("nodes", None),
        ),
        out_specs=(P("feat", "nodes"), P(None, "feat"), P("feat", "nodes")),
        check_vma=False,
    )
```

```python
import jax
import jax.numpy as jnp
from jax import lax
from jax.experimental import pallas as pl
from jax.experimental.pallas import tpu as pltpu
from jax.sharding import PartitionSpec as P

BF = jnp.bfloat16
F32 = jnp.float32


def silu_slope(pre):
    sig = jax.nn.sigmoid(pre)
    return sig * (1.0 + pre * (1.0 - sig))


def swap(values):
    return lax.all_to_all(values, "nodes", split_axis=0, concat_axis=0, tiled=True)


def trade(values, step):
    count = lax.axis_size("feat")
    return lax.ppermute(values, "feat", [(i, i ^ step) for i in range(count)])


def spread(piece, axes):
    count = 1
    for name in axes:
        count = count * lax.axis_size(name)
    pieces = jnp.broadcast_to(piece[None], (count,) + piece.shape)
    return lax.all_to_all(pieces, axes, split_axis=0, concat_axis=0, tiled=True)


TAIL = 8
SMEM = pl.BlockSpec(memory_space=pltpu.SMEM)
VMEM = pl.BlockSpec(memory_space=pltpu.VMEM)


def pack_kernel(sends_ref, hubs_ref, x_hbm, msg_ref, x_ref, tail_ref, sem):
    load = pltpu.make_async_copy(x_hbm, x_ref, sem)
    load.start()
    me = lax.axis_index("nodes")
    quarter = x_ref.shape[0]
    count, rows, block_len = msg_ref.shape
    blk_count = x_ref.shape[1] // block_len
    per_dev = (rows - TAIL) // quarter
    hubs = hubs_ref.shape[0]
    share = hubs * quarter // count

    def columns(block):
        return pl.ds(pl.multiple_of(block * block_len, block_len), block_len)

    def one(r, carry):
        for k in range(per_dev):
            block = sends_ref[k, r]
            msg_ref[r, k * quarter : (k + 1) * quarter, :] = x_ref[:, columns(block)]
        return carry

    tail_ref[...] = jnp.zeros_like(tail_ref)
    load.wait()
    lax.fori_loop(0, count, one, 0, unroll=count)
    for h in range(hubs):
        local = hubs_ref[h] - me * blk_count
        inside = (local >= 0) & (local < blk_count)
        values = x_ref[:, columns(jnp.clip(local, 0, blk_count - 1))].astype(F32)
        values = jnp.where(inside, values, 0.0)
        for i in range(quarter // share):
            place = h * (quarter // share) + i
            tail_ref[place, :share, :] = values[i * share : (i + 1) * share]
    msg_ref[:, per_dev * quarter :, :] = tail_ref[...].astype(BF)


def pack(sends, hub_ids, x_t, count, per_dev, block_len):
    rows = per_dev * x_t.shape[0] + TAIL
    return pl.pallas_call(
        pack_kernel,
        out_shape=jax.ShapeDtypeStruct((count, rows, block_len), BF),
        in_specs=[SMEM, SMEM, pl.BlockSpec(memory_space=pl.ANY)],
        out_specs=VMEM,
        scratch_shapes=[
            pltpu.VMEM(x_t.shape, x_t.dtype),
            pltpu.VMEM((count, TAIL, block_len), F32),
            pltpu.SemaphoreType.DMA,
        ],
        compiler_params=pltpu.CompilerParams(vmem_limit_bytes=56 << 20),
        name="pack",
    )(sends, hub_ids, x_t)


def middle_kernel(row_ref, hub_ref, p0, p1, p2, p3, weight_ref, cot_ref, act_ref, out_ref):
    parts = (p0, p1, p2, p3)
    blks, quarter, block_len = p0.shape
    hid = weight_ref.shape[0] // len(parts)
    weight = weight_ref[...]
    total = jnp.zeros((weight.shape[0], weight.shape[1]), F32)
    for b in range(blks):
        columns = slice(b * block_len, (b + 1) * block_len)
        agg = []
        for k, part in enumerate(parts):
            first = pl.multiple_of((row_ref[0] ^ k) * quarter, quarter)
            agg.append(part[b].astype(F32) + hub_ref[b, pl.ds(first, quarter), :])
        agg = jnp.concatenate(agg, axis=0).astype(BF)
        pre = jnp.dot(weight, agg, preferred_element_type=F32)
        sig = jax.nn.sigmoid(pre)
        act_ref[:, columns] = (pre * sig).astype(BF)
        slope = sig * (1.0 + pre * (1.0 - sig))
        pre_grad = (cot_ref[:, columns].astype(F32) * slope).astype(BF)
        agg_grad = lax.dot_general(
            weight, pre_grad, (((0,), (0,)), ((), ())), preferred_element_type=F32
        ).astype(BF)
        for k in range(len(parts)):
            out_ref[k, b * quarter : (b + 1) * quarter, :] = agg_grad[k * quarter : (k + 1) * quarter]
        total = total + lax.dot_general(
            pre_grad, agg, (((1,), (1,)), ((), ())), preferred_element_type=F32
        )
    total = total.astype(BF)
    for k in range(len(parts)):
        out_ref[k, blks * quarter :, :] = total[k * hid : (k + 1) * hid]


def middle(row, hub_agg, parts, weight, cot):
    blks, quarter, block_len = parts[0].shape
    hid = weight.shape[0] // len(parts)
    return pl.pallas_call(
        middle_kernel,
        out_shape=[
            jax.ShapeDtypeStruct(cot.shape, BF),
            jax.ShapeDtypeStruct((len(parts), blks * quarter + hid, block_len), BF),
        ],
        in_specs=[SMEM] + [VMEM] * (3 + len(parts)),
        out_specs=[VMEM, VMEM],
        compiler_params=pltpu.CompilerParams(vmem_limit_bytes=16 << 20),
        cost_estimate=pl.CostEstimate(flops=6 * weight.size * cot.shape[1], transcendentals=cot.size, bytes_accessed=2 << 20),
        name="middle",
    )(row, hub_agg, *parts, weight, cot)


def finish_kernel(hubs_ref, own_ref, sums_ref, grad_ref, weight_ref, hub_ref):
    quarter = own_ref.shape[0]
    hubs, block_len = hub_ref.shape[0], hub_ref.shape[2]
    blk_count = own_ref.shape[1] // block_len
    count = sums_ref.shape[0]
    share = hubs * quarter // count
    for place in range(count):
        h, i = divmod(place, quarter // share)
        piece = sums_ref[place].astype(F32)
        hub_ref[h, i * share : (i + 1) * share, :] = piece[:share]
        weight_ref[place : place + 1, :] = piece[share : share + 1]
    grad_ref[...] = own_ref[...]
    for h in range(hubs):
        local = hubs_ref[h]

        @pl.when((local >= 0) & (local < blk_count))
        def _():
            first = jnp.clip(local, 0, blk_count - 1) * block_len
            columns = pl.ds(pl.multiple_of(first, block_len), block_len)
            grad_ref[:, columns] += hub_ref[h]


def finish(hubs_here, own, sums, quarter, hid, block_len):
    return pl.pallas_call(
        finish_kernel,
        out_shape=[
            jax.ShapeDtypeStruct(own.shape, F32),
            jax.ShapeDtypeStruct((hid, block_len), F32),
        ],
        in_specs=[SMEM, VMEM, VMEM],
        out_specs=[VMEM, VMEM],
        scratch_shapes=[pltpu.VMEM((hubs_here.shape[0], quarter, block_len), F32)],
        compiler_params=pltpu.CompilerParams(vmem_limit_bytes=16 << 20),
        name="finish",
    )(hubs_here, own, sums)


def per_device(
    x_t, weight, cotangent, self_tiles, hub_tiles, nbr_tiles, hub_ids, send_list, nbr_slot
):
    quarter = x_t.shape[0]
    blk_count, block_len = self_tiles.shape[0], self_tiles.shape[1]
    hubs, nbrs = hub_tiles.shape[1], nbr_tiles.shape[1]
    hid = weight.shape[1]
    count = lax.axis_size("nodes")
    feats = lax.axis_size("feat")
    row = lax.axis_index("feat")
    me = lax.axis_index("nodes")
    sends = send_list[0].reshape(-1)
    slots = nbr_slot[0]
    per_pair = 2 * quarter
    blk_share = blk_count // feats
    share = blk_share * block_len
    steps = jnp.arange(feats, dtype=jnp.int32)

    ids = jnp.arange(blk_count, dtype=jnp.int32)
    hubs_here = hub_ids - me * blk_count
    per_dev = send_list.shape[2]
    got = swap(pack(send_list[0].T, hub_ids, x_t, count, per_dev, block_len))

    cot = cotangent.reshape(hid, feats, share)
    cot_parts, weight_parts = [], []
    for k in range(feats):
        part = lax.dynamic_index_in_dim(cot, row ^ k, 1, keepdims=False)
        part = jnp.concatenate([part, weight.T], axis=1)
        part = trade(part, k) if k else part
        cot_parts.append(part[:, :share])
        weight_parts.append(part[:, share:])
    cot_share = jnp.concatenate(cot_parts, axis=0)
    turned = jnp.concatenate(weight_parts, axis=0).reshape(feats * hid, feats, quarter)
    turned = jnp.take(turned, row ^ steps, axis=1, mode="clip")
    feat_ids = jnp.arange(feats * quarter, dtype=jnp.int32)
    owner = row ^ steps[:, None] ^ (feat_ids[None, :] // quarter)
    source = feat_ids[None, :] % quarter + owner * quarter
    unturn = (source[:, None, :] == feat_ids[None, :, None]).astype(BF)

    got, slots, sends, x_t, hubs_here, turned, cot_share, unturn = lax.optimization_barrier(
        (got, slots, sends, x_t, hubs_here, turned, cot_share, unturn)
    )
    blocks = x_t.reshape(quarter, blk_count, block_len).transpose(1, 0, 2)
    hub_rows = hubs * quarter // count
    hub_piece = jnp.sum(got[:, per_pair : per_pair + hub_rows].astype(F32), axis=0).astype(BF)
    hub_x = spread(hub_piece, ("nodes", "feat")).reshape(count, feats, hub_rows, block_len)
    hub_x = hub_x.transpose(1, 0, 2, 3).reshape(feats, hubs, quarter, block_len)

    slot_x = got[:, :per_pair].reshape(-1, quarter, block_len)
    chosen = jnp.take(slot_x, slots, axis=0, mode="clip")
    chosen = chosen.reshape(blk_count, nbrs, quarter, block_len)
    total = jnp.einsum("bjfs,bjsd->bfd", chosen, nbr_tiles, preferred_element_type=F32)
    total = total + jnp.einsum("bfs,bsd->bfd", blocks, self_tiles, preferred_element_type=F32)
    total = total.astype(BF).reshape(feats, blk_share, quarter, block_len)
    parts = []
    for k in range(feats):
        part = lax.dynamic_index_in_dim(total, row ^ k, 0, keepdims=False)
        parts.append(trade(part, k) if k else part)
    hub_share = lax.dynamic_slice_in_dim(hub_tiles, row * blk_share, blk_share, axis=0)
    hub_agg = jnp.einsum("ghfs,bhsd->bgfd", hub_x, hub_share, preferred_element_type=F32)
    hub_agg = hub_agg.reshape(blk_share, feats * quarter, block_len)
    act, message = middle(row.reshape(1), hub_agg, parts, turned.reshape(feats * hid, feats * quarter), cot_share)
    messages = [message[0]] + [trade(message[k], k) for k in range(1, feats)]
    message = jnp.stack(messages)
    upstream = []
    for q in range(feats):
        share_of_q = messages[0][: blk_share * quarter]
        for k in range(1, feats):
            share_of_q = jnp.where(row == q ^ k, messages[k][: blk_share * quarter], share_of_q)
        upstream.append(share_of_q)
    upstream = jnp.concatenate(upstream, axis=0).reshape(blk_count, quarter, block_len)
    weight_sum = jnp.einsum(
        "khe,kef->hf", message[:, blk_share * quarter :], unturn, preferred_element_type=F32
    )

    near = jnp.einsum("bfd,bjsd->bjfs", upstream, nbr_tiles, preferred_element_type=F32)
    near = near.astype(BF).reshape(blk_count * nbrs, quarter, block_len)
    tile_of = jnp.zeros_like(slots).at[slots].set(jnp.arange(slots.shape[0], dtype=slots.dtype))
    placed = jnp.take(near, tile_of, axis=0, mode="clip").reshape(count, per_pair, block_len)
    hub_terms = jnp.einsum("bfd,bhsd->hfs", upstream, hub_tiles, preferred_element_type=F32)
    hub_terms = hub_terms.astype(BF).reshape(count, -1, block_len)
    weight_sum = weight_sum.astype(BF).reshape(count, -1, block_len)
    back = swap(jnp.concatenate([placed, hub_terms, weight_sum], axis=1))

    act = act.reshape(feats, hid, share)
    acts = [act[0]] + [trade(act[k], k) for k in range(1, feats)]
    activation = jnp.take(jnp.stack(acts, axis=1), row ^ steps, axis=1, mode="clip")
    activation = activation.reshape(hid, blk_count * block_len)

    sums = jnp.sum(back[:, per_pair : per_pair + hub_rows + 1].astype(F32), axis=0)
    sums = spread(sums.astype(BF), ("nodes",))
    returned = back[:, :per_pair].reshape(-1, quarter, block_len)
    own = jnp.einsum("bfd,bsd->bfs", upstream, self_tiles, preferred_element_type=F32)
    send_select = (sends[:, None] == ids[None, :]).astype(BF)
    own = own + jnp.einsum("rfs,rb->bfs", returned, send_select, preferred_element_type=F32)
    own = own.transpose(1, 0, 2).reshape(quarter, blk_count * block_len)
    input_grad, weight_grad = finish(hubs_here, own, sums, quarter, hid, block_len)
    return (activation, weight_grad.T, input_grad)


def solution(mesh):
    return jax.shard_map(
        per_device,
        mesh=mesh,
        in_specs=(
            P("feat", "nodes"),
            P(None, "feat"),
            P("feat", "nodes"),
            P("nodes", None, None),
            P("nodes", None, None, None),
            P("nodes", None, None, None),
            P(),
            P("nodes", None, None),
            P("nodes", None),
        ),
        out_specs=(P("feat", "nodes"), P(None, "feat"), P("feat", "nodes")),
        check_vma=False,
    )
```
